32 devices in a mesh: row: 2 (over x), col: 16 (over z, y, core).
Axes of the slice: x: 2, y: 2, z: 4, core: 2. Of those that a mesh axis runs over, the one named last changes fastest.
Arguments:
- region_factors: bfloat16 [32768, 512], P(('row', 'col')), may hold values from -1.25 to 1.25
- item_factors: bfloat16 [16, 128, 512], P('col', 'row'), may hold values from -1.25 to 1.25
- slab_blocks: bfloat16 [32, 16, 6, 128, 128], P(('row', 'col')), may hold values from -6 to 6
- block_rows: int32 [32, 16, 6], P(('row', 'col')), may hold values from 0 to 7, as said below
- counts: int32 [32, 16], P(('row', 'col')), may hold values from 1 to 6, as said below
Outputs:
- new_regions: float32 [32768, 512], P(('row', 'col'))
- new_items: float32 [16, 128, 512], P('col', 'row')
The draws below stay inside these ranges and needn't reach their ends.
Inputs may be any that keep to these rules, and one draw needn't show every extreme that they name: `counts`: every entry is at least 1; some device-block has exactly 6 present blocks in some block column. `block_rows`: for each device-block and block column, the first counts[d, p] entries are distinct; entries at slots s >= counts[d, p] (and their slab blocks) are not used.
All inputs are finite; a program needn't handle non-finite values.
Results may differ from the reference program's by a relative error of at most 0.0023.
Values may be sent and summed in bfloat16 or wider, within the bound.
A program may use at most 128 MiB of HBM per device.

```python
import jax
import jax.numpy as jnp
from jax import lax

RANK = 512
BLOCK = 128
RB_DEV = 8
PCAP = 6
PANELS = 16
REGIONS = 32768
DEVICES = 32


def draw_block_rows(key, part):
    key_rows = jax.random.fold_in(key, 17)
    scores = jax.random.randint(key_rows, (DEVICES, PANELS, RB_DEV), 0, 1 << 20) * RB_DEV
    scores = scores + jnp.arange(RB_DEV, dtype=jnp.int32)
    ranking = jnp.argsort(scores, axis=-1)
    return ranking[:, :, :PCAP].astype(jnp.int32)


def draw_counts(key, part):
    key_counts = jax.random.fold_in(key, 29)
    key_level, key_drawn, key_device, key_column = jax.random.split(key_counts, 4)
    density = jax.random.randint(key_level, (DEVICES, 1), 1, PCAP + 1)
    drawn = jax.random.randint(key_drawn, (DEVICES, PANELS), 1, density + 1)
    busy_device = jax.random.randint(key_device, (), 0, DEVICES)
    busy_column = jax.random.randint(key_column, (), 0, PANELS)
    chosen_cell = (jnp.arange(DEVICES, dtype=jnp.int32)[:, None] == busy_device) & (jnp.arange(PANELS, dtype=jnp.int32)[None, :] == busy_column)
    return jnp.where(chosen_cell, PCAP, drawn).astype(jnp.int32)


def levels(own_key, dims, pieces, low, high):
    def one(position, blocks):
        heights = jax.random.uniform(jax.random.fold_in(jax.random.fold_in(own_key, 6), position), (blocks,), jnp.float32, low / len(pieces), high / len(pieces))
        return jnp.repeat(jnp.exp(heights), dims[position] // blocks).reshape((-1,) + (1,) * (len(dims) - position - 1))

    level = one(*pieces[0])
    for cut in pieces[1:]:
        level = level * one(*cut)
    return level


def normal_values(rng, extent, scale, most, pieces=(), kind=jnp.bfloat16):
    array = scale * jax.random.normal(rng, extent, jnp.float32)
    if pieces:
        array = array * levels(rng, extent, pieces, -0.22, 0.18)
    return jnp.clip(array, -most, most).astype(kind)


def setup_inputs(seed: int = 0) -> dict:
    key_list = jax.random.split(jax.random.key(seed), 6)
    return {
        "region_factors": normal_values(key_list[0], (REGIONS, RANK), (RANK ** -0.25), 1.25, ((0, 32),)),
        "item_factors": normal_values(key_list[1], (PANELS, BLOCK, RANK), (RANK ** -0.25), 1.25, ((0, 16), (1, 2))),
        "slab_blocks": normal_values(key_list[2], (DEVICES, PANELS, PCAP, BLOCK, BLOCK), 1.0, 6.0, ((0, 32),)),
        "block_rows": draw_block_rows(jax.random.fold_in(key_list[5], 71), 0),
        "counts": draw_counts(jax.random.fold_in(key_list[5], 71), 0),
    }


region_rate = 0.05
item_rate = 0.01
decay_rate = 0.1


def reference(region_factors, item_factors, slab_blocks, block_rows, counts):
    items_wide = item_factors.astype(jnp.float32)
    slot_ids = jnp.arange(PCAP, dtype=jnp.int32)
    block_ids = jnp.arange(RB_DEV, dtype=jnp.int32)
    region_blocks = region_factors.reshape(DEVICES, RB_DEV, BLOCK, RANK)

    def per_device(carried, inputs):
        device_rows, device_tiles, device_lists, device_counts = inputs
        present = slot_ids[None, :] < device_counts[:, None]
        chosen = device_rows[device_lists].astype(jnp.float32)
        predicted = jnp.einsum("psik,pjk->psij", chosen, items_wide)
        residual = jnp.where(present[:, :, None, None], predicted - device_tiles.astype(jnp.float32), 0.0)
        residual = residual.astype(jnp.bfloat16).astype(jnp.float32)
        terms = jnp.einsum("psij,pjk->psik", residual, items_wide)
        selector = (device_lists[:, :, None] == block_ids[None, None, :]).astype(jnp.float32)
        region_part = jnp.einsum("psr,psik->rik", selector, terms)
        carried = carried + jnp.einsum("psij,psik->pjk", residual, chosen)
        return carried, region_part

    item_grad, region_grad = lax.scan(
        per_device,
        jnp.zeros((PANELS, BLOCK, RANK), jnp.float32),
        (region_blocks, slab_blocks, block_rows, counts),
    )
    region_grad = region_grad.reshape(REGIONS, RANK)
    regions_wide = region_factors.astype(jnp.float32)
    new_regions = regions_wide - region_rate * (region_grad + decay_rate * regions_wide)
    new_items = items_wide - item_rate * (item_grad + decay_rate * items_wide)
    return new_regions, new_items
```

```python
import functools

import jax
import jax.numpy as jnp
from jax import lax
from jax.experimental import pallas as pl
from jax.experimental.pallas import tpu as pltpu
from jax.sharding import PartitionSpec as P

region_rate = 0.05
item_rate = 0.01
decay_rate = 0.1

MESH = pl.DeviceIdType.MESH
CORES = 2
NT = (((1,), (1,)), ((), ()))
TN = (((0,), (0,)), ((), ()))
NN = (((1,), (0,)), ((), ()))


def mm(a, b, dims):
    return lax.dot_general(a, b, dims, preferred_element_type=jnp.float32)


def kernel(R, Z, Y, chunk, items, regions, slab, rows, counts, new_regions, new_items,
           u, tiles, v, res, racc, gown, gsend, grecv,
           s_a, r_a, s_b, r_b, s_x, r_x, s_y, r_y, s_z, r_z, acc,
           loc_sem, out_sem, az, ax, ay, aa, ab, sib, gc, ga, gb, gx, gy, gz):
    x = lax.axis_index("row")
    c = lax.axis_index("col")
    k = lax.rem(c, CORES)
    y = lax.rem(c // CORES, Y)
    z = c // (CORES * Y)
    block = tiles.shape[-1]
    width = u.shape[-1]
    half = width // 2
    n = block // R
    slots = tiles.shape[1]
    chunks = u.shape[0] // chunk

    def col_of(zz, yy, kk):
        return (zz * Y + yy) * CORES + kk

    def xdev(d):
        return {"row": lax.rem(x + d, R), "col": c}

    def ydev(d):
        return {"row": x, "col": col_of(z, lax.rem(y + d, Y), k)}

    def zdev(d):
        return {"row": x, "col": col_of(lax.rem(z + d, Z), y, k)}

    sibling = {"row": x, "col": col_of(z, y, 1 - k)}
    peers = [xdev(d) for d in range(1, R)] + [ydev(d) for d in range(1, Y)] + [zdev(d) for d in range(1, Z)] + [sibling]

    load_u = pltpu.make_async_copy(regions, u, loc_sem.at[0])
    load_u.start()
    load_tiles = pltpu.make_async_copy(slab.at[0], tiles, loc_sem.at[1])
    load_tiles.start()

    barrier = pltpu.get_barrier_semaphore()
    for peer in peers:
        pl.semaphore_signal(barrier, inc=1, device_id=peer, device_id_type=MESH)
    pl.semaphore_wait(barrier, len(peers))

    sent = []

    def remote(src, dst, sems, index, device):
        return pltpu.make_async_remote_copy(
            src_ref=src, dst_ref=dst, send_sem=sems.at[(0,) + index], recv_sem=sems.at[(1,) + index],
            device_id=device, device_id_type=MESH)

    def send(src, dst, sems, index, device):
        copy = remote(src, dst, sems, index, device)
        copy.start()
        sent.append(copy)

    def arrived(dst, sems, index):
        remote(dst, dst, sems, index, sibling).wait_recv()

    def zslot(j):
        return lax.rem(z + j, Z)

    def xback(d):
        return lax.rem(x + R - d, R)

    def yback(d):
        return lax.rem(y + Y - d, Y)

    def at_row(yy, xx):
        return pl.ds(pl.multiple_of(yy * block + xx * n, n), n)

    def piece(j, yy, xx, columns=slice(None)):
        return v.at[zslot(j), k, at_row(yy, xx), columns]

    first, second = pl.ds(0, half), pl.ds(half, half)

    def plane_start(j):
        own = piece(j, y, x)
        for d in range(1, R):
            send(own, own, ax, (j, d), xdev(d))
        for d in range(1, Y):
            send(own, own, ay, (j, d), ydev(d))

    def forward(j):
        for dx in range(1, R):
            arrived(piece(j, y, xback(dx)), ax, (j, dx))
            part = piece(j, y, xback(dx), first)
            for dy in range(1, Y):
                send(part, part, aa, (j, dx, dy), ydev(dy))
        for dy in range(1, Y):
            arrived(piece(j, yback(dy), x), ay, (j, dy))
            part = piece(j, yback(dy), x, second)
            for dx in range(1, R):
                send(part, part, ab, (j, dx, dy), xdev(dx))

    def share(j):
        for dx in range(1, R):
            for dy in range(1, Y):
                arrived(piece(j, yback(dy), xback(dx), first), aa, (j, dx, dy))
                arrived(piece(j, yback(dy), xback(dx), second), ab, (j, dx, dy))
        mine = v.at[zslot(j), k]
        send(mine, mine, sib, (j,), sibling)

    def shared(j):
        arrived(v.at[zslot(j), 1 - k], sib, (j,))

    def residuals(j):
        zz = zslot(j)

        def body(i, carry):
            start = pl.multiple_of(i * chunk, chunk)
            u_now = u[pl.ds(start, chunk), :]
            for o in range(CORES):
                kk = lax.rem(k + o, CORES)
                predicted = mm(u_now, v[zz, kk], NT)
                for yy in range(Y):
                    p = col_of(zz, yy, kk)
                    count = counts[0, p]
                    for part in range(chunk // block):
                        b = i * (chunk // block) + part
                        found = jnp.int32(0)
                        for s in range(slots):
                            hit = (rows[0, p, s] == b) & (count > s)
                            found = jnp.where(hit, s + 1, found)
                        live = jnp.where(found > 0, jnp.float32(1), jnp.float32(0))
                        tile = tiles[p, jnp.maximum(found - 1, 0)].astype(jnp.float32)
                        pred = predicted[part * block:(part + 1) * block, yy * block:(yy + 1) * block]
                        res[o, pl.ds(pl.multiple_of(start + part * block, block), block), yy * block:(yy + 1) * block] = (
                            (pred - tile) * live).astype(jnp.bfloat16)
            return carry

        lax.fori_loop(0, chunks, body, 0)

    def region_part(j):
        zz = zslot(j)

        def body(i, carry):
            here = pl.ds(pl.multiple_of(i * chunk, chunk), chunk)
            total = mm(res[0, here, :], v[zz, k], NN) + mm(res[1, here, :], v[zz, 1 - k], NN)
            if j > 0:
                total = total + racc[here, :]
            if j == Z - 1:
                wide = u[here, :].astype(jnp.float32)
                total = wide - region_rate * (total + decay_rate * wide)
            racc[here, :] = total
            if j == Z - 1:
                pltpu.make_async_copy(racc.at[here, :], new_regions.at[here, :], out_sem.at[i]).start()
            return carry

        lax.fori_loop(0, chunks, body, 0)

    def reduce_first(j):
        arrived(grecv.at[j], gc, (j,))
        gown[j] = gown[j] + grecv[j]
        for dy in range(1, Y):
            yy = lax.rem(y + dy, Y)
            for dx in range(1, R):
                s_a[j, dy - 1, (dx - 1) * n:dx * n, :] = gown[j, at_row(yy, lax.rem(x + dx, R)), :half].astype(jnp.bfloat16)
            send(s_a.at[j, dy - 1], r_a.at[j, dy - 1], ga, (j, dy), ydev(dy))
        for dx in range(1, R):
            xx = lax.rem(x + dx, R)
            for dy in range(1, Y):
                s_b[j, dx - 1, (dy - 1) * n:dy * n, :] = gown[j, at_row(lax.rem(y + dy, Y), xx), half:].astype(jnp.bfloat16)
            send(s_b.at[j, dx - 1], r_b.at[j, dx - 1], gb, (j, dx), xdev(dx))

    def reduce_second(j):
        for dy in range(1, Y):
            arrived(r_a.at[j, dy - 1], ga, (j, dy))
        for dx in range(1, R):
            here = at_row(y, lax.rem(x + dx, R))
            total = gown[j, here, :half]
            for dy in range(1, Y):
                total = total + r_a[j, dy - 1, (dx - 1) * n:dx * n, :].astype(jnp.float32)
            s_x[j, dx - 1, :, :half] = total.astype(jnp.bfloat16)
            s_x[j, dx - 1, :, half:] = gown[j, here, half:].astype(jnp.bfloat16)
            send(s_x.at[j, dx - 1], r_x.at[j, dx - 1], gx, (j, dx), xdev(dx))
        for dx in range(1, R):
            arrived(r_b.at[j, dx - 1], gb, (j, dx))
        for dy in range(1, Y):
            here = at_row(lax.rem(y + dy, Y), x)
            total = gown[j, here, half:]
            for dx in range(1, R):
                total = total + r_b[j, dx - 1, (dy - 1) * n:dy * n, :].astype(jnp.float32)
            s_y[j, dy - 1, :, half:] = total.astype(jnp.bfloat16)
            s_y[j, dy - 1, :, :half] = gown[j, here, :half].astype(jnp.bfloat16)
            send(s_y.at[j, dy - 1], r_y.at[j, dy - 1], gy, (j, dy), ydev(dy))

    def reduce_third(j):
        total = gown[j, at_row(y, x), :]
        for dx in range(1, R):
            arrived(r_x.at[j, dx - 1], gx, (j, dx))
            total = total + r_x[j, dx - 1].astype(jnp.float32)
        for dy in range(1, Y):
            arrived(r_y.at[j, dy - 1], gy, (j, dy))
            total = total + r_y[j, dy - 1].astype(jnp.float32)
        if j == 0:
            acc[...] = total
        else:
            s_z[j - 1] = total.astype(jnp.bfloat16)
            send(s_z.at[j - 1], r_z.at[j - 1], gz, (j,), zdev(j))

    v[z, k, at_row(y, x), :] = items[0]
    own = piece(0, y, x)
    plane_start(0)
    for d in range(1, Z):
        send(own, own, az, (d,), zdev(d))
    for j in range(1, Z):
        arrived(piece(j, y, x), az, (Z - j,))
        plane_start(j)
    forward(0)
    for j in range(Z):
        if j + 1 < Z:
            forward(j + 1)
        share(j)
        shared(j)
        if j == 0:
            load_u.wait()
            load_tiles.wait()
        residuals(j)
        gsend[j] = mm(res[1], u[...], TN)
        send(gsend.at[j], grecv.at[j], gc, (j,), sibling)
        if j > 0:
            reduce_second(j - 1)
        gown[j] = mm(res[0], u[...], TN)
        region_part(j)
        reduce_first(j)
        if j > 0:
            reduce_third(j - 1)
    reduce_second(Z - 1)
    reduce_third(Z - 1)
    total = acc[...]
    for j in range(1, Z):
        arrived(r_z.at[j - 1], gz, (j,))
        total = total + r_z[j - 1].astype(jnp.float32)
    wide = items[0].astype(jnp.float32)
    new_items[0] = wide - item_rate * (total + decay_rate * wide)
    for copy in sent:
        copy.wait_send()

    def finish(i, carry):
        here = pl.ds(pl.multiple_of(i * chunk, chunk), chunk)
        pltpu.make_async_copy(racc.at[here, :], new_regions.at[here, :], out_sem.at[i]).wait()
        return carry

    lax.fori_loop(0, chunks, finish, 0)


def on_device(R, Z, Y, region_factors, item_factors, slab_blocks, block_rows, counts):
    bf16, f32 = jnp.bfloat16, jnp.float32
    height, width = region_factors.shape
    _, panels, slots, block, _ = slab_blocks.shape
    n, half, side = block // R, width // 2, Y * block
    chunk = 2 * block
    dma = pltpu.SemaphoreType.DMA
    vmem = pltpu.VMEM
    return pl.pallas_call(
        functools.partial(kernel, R, Z, Y, chunk),
        out_shape=(jax.ShapeDtypeStruct((height, width), f32), jax.ShapeDtypeStruct(item_factors.shape, f32)),
        in_specs=[
            pl.BlockSpec(memory_space=pltpu.VMEM),
            pl.BlockSpec(memory_space=pl.ANY),
            pl.BlockSpec(memory_space=pl.ANY),
            pl.BlockSpec(memory_space=pltpu.SMEM),
            pl.BlockSpec(memory_space=pltpu.SMEM),
        ],
        out_specs=(pl.BlockSpec(memory_space=pl.ANY), pl.BlockSpec(memory_space=pltpu.VMEM)),
        scratch_shapes=[
            vmem((height, width), bf16),
            vmem((panels, slots, block, block), bf16),
            vmem((Z, CORES, side, width), bf16),
            vmem((CORES, height, side), bf16),
            vmem((height, width), f32),
            vmem((Z, side, width), f32),
            vmem((Z, side, width), f32),
            vmem((Z, side, width), f32),
            vmem((Z, Y - 1, (R - 1) * n, half), bf16),
            vmem((Z, Y - 1, (R - 1) * n, half), bf16),
            vmem((Z, R - 1, (Y - 1) * n, half), bf16),
            vmem((Z, R - 1, (Y - 1) * n, half), bf16),
            vmem((Z, R - 1, n, width), bf16),
            vmem((Z, R - 1, n, width), bf16),
            vmem((Z, Y - 1, n, width), bf16),
            vmem((Z, Y - 1, n, width), bf16),
            vmem((Z - 1, n, width), bf16),
            vmem((Z - 1, n, width), bf16),
            vmem((n, width), f32),
            dma((2,)),
            dma((height // chunk,)),
            dma((2, Z)),
            dma((2, Z, R)),
            dma((2, Z, Y)),
            dma((2, Z, R, Y)),
            dma((2, Z, R, Y)),
            dma((2, Z)),
            dma((2, Z)),
            dma((2, Z, Y)),
            dma((2, Z, R)),
            dma((2, Z, R)),
            dma((2, Z, Y)),
            dma((2, Z)),
        ],
        compiler_params=pltpu.CompilerParams(
            collective_id=0, has_side_effects=True, vmem_limit_bytes=56 * 1024 * 1024),
        cost_estimate=pl.CostEstimate(
            flops=6 * height * panels * block * width, bytes_accessed=8 * height * width, transcendentals=0),
    )(item_factors, region_factors, slab_blocks, block_rows, counts)


def solution(mesh):
    R, C = mesh.shape["row"], mesh.shape["col"]
    chips = C // CORES
    Z = 4
    Y = chips // Z
    return jax.shard_map(
        functools.partial(on_device, R, Z, Y),
        mesh=mesh,
        in_specs=(
            P(("row", "col"), None),
            P("col", "row", None),
            P(("row", "col"), None, None, None, None),
            P(("row", "col"), None, None),
            P(("row", "col"), None),
        ),
        out_specs=(P(("row", "col"), None), P("col", "row", None)),
        check_vma=False,
    )
```

```python
import functools

import jax
import jax.numpy as jnp
from jax import lax
from jax.experimental import pallas as pl
from jax.experimental.pallas import tpu as pltpu
from jax.sharding import PartitionSpec as P

region_rate = 0.05
item_rate = 0.01
decay_rate = 0.1

MESH = pl.DeviceIdType.MESH
CORES = 2
NT = (((1,), (1,)), ((), ()))
TN = (((0,), (0,)), ((), ()))
NN = (((1,), (0,)), ((), ()))


def mm(a, b, dims):
    return lax.dot_general(a, b, dims, preferred_element_type=jnp.float32)


def kernel(R, Z, Y, chunk, items, regions, slab, rows, counts, region_grad, new_items,
           u, tiles, v, res, racc, gown, gsend, grecv,
           s_a, r_a, s_b, r_b, s_x, r_x, s_y, r_y, s_z, r_z, acc,
           loc_sem, out_sem, az, ax, ay, aa, ab, sib, gc, ga, gb, gx, gy, gz):
    x = lax.axis_index("row")
    c = lax.axis_index("col")
    k = lax.rem(c, CORES)
    y = lax.rem(c // CORES, Y)
    z = c // (CORES * Y)
    block = tiles.shape[-1]
    width = u.shape[-1]
    half = width // 2
    n = block // R
    slots = tiles.shape[1]
    chunks = u.shape[0] // chunk

    def col_of(zz, yy, kk):
        return (zz * Y + yy) * CORES + kk

    def xdev(d):
        return {"row": lax.rem(x + d, R), "col": c}

    def ydev(d):
        return {"row": x, "col": col_of(z, lax.rem(y + d, Y), k)}

    def zdev(d):
        return {"row": x, "col": col_of(lax.rem(z + d, Z), y, k)}

    sibling = {"row": x, "col": col_of(z, y, 1 - k)}
    peers = [xdev(d) for d in range(1, R)] + [ydev(d) for d in range(1, Y)] + [zdev(d) for d in range(1, Z)] + [sibling]

    load_u = pltpu.make_async_copy(regions, u, loc_sem.at[0])
    load_u.start()
    load_tiles = pltpu.make_async_copy(slab.at[0], tiles, loc_sem.at[1])
    load_tiles.start()

    barrier = pltpu.get_barrier_semaphore()
    for peer in peers:
        pl.semaphore_signal(barrier, inc=1, device_id=peer, device_id_type=MESH)
    pl.semaphore_wait(barrier, len(peers))

    sent = []

    def remote(src, dst, sems, index, device):
        return pltpu.make_async_remote_copy(
            src_ref=src, dst_ref=dst, send_sem=sems.at[(0,) + index], recv_sem=sems.at[(1,) + index],
            device_id=device, device_id_type=MESH)

    def send(src, dst, sems, index, device):
        copy = remote(src, dst, sems, index, device)
        copy.start()
        sent.append(copy)

    def arrived(dst, sems, index):
        remote(dst, dst, sems, index, sibling).wait_recv()

    def zslot(j):
        return lax.rem(z + j, Z)

    def xback(d):
        return lax.rem(x + R - d, R)

    def yback(d):
        return lax.rem(y + Y - d, Y)

    side = Y * block

    def at_row(yy, xx):
        return pl.ds(pl.multiple_of(yy * block + xx * n, n), n)

    def core_rows(kk):
        return pl.ds(pl.multiple_of(kk * side, side), side)

    def piece(j, yy, xx, columns=slice(None)):
        return v.at[zslot(j), pl.ds(pl.multiple_of(k * side + yy * block + xx * n, n), n), columns]

    first, second = pl.ds(0, half), pl.ds(half, half)

    def plane_start(j):
        own = piece(j, y, x)
        for d in range(1, R):
            send(own, own, ax, (j, d), xdev(d))
        for d in range(1, Y):
            send(own, own, ay, (j, d), ydev(d))

    def forward(j):
        for dx in range(1, R):
            arrived(piece(j, y, xback(dx)), ax, (j, dx))
            part = piece(j, y, xback(dx), first)
            for dy in range(1, Y):
                send(part, part, aa, (j, dx, dy), ydev(dy))
        for dy in range(1, Y):
            arrived(piece(j, yback(dy), x), ay, (j, dy))
            part = piece(j, yback(dy), x, second)
            for dx in range(1, R):
                send(part, part, ab, (j, dx, dy), xdev(dx))

    def share(j):
        for dx in range(1, R):
            for dy in range(1, Y):
                arrived(piece(j, yback(dy), xback(dx), first), aa, (j, dx, dy))
                arrived(piece(j, yback(dy), xback(dx), second), ab, (j, dx, dy))
        mine = v.at[zslot(j), core_rows(k)]
        send(mine, mine, sib, (j,), sibling)

    def shared(j):
        arrived(v.at[zslot(j), core_rows(1 - k)], sib, (j,))

    def residuals(j):
        zz = zslot(j)

        def body(i, carry):
            start = pl.multiple_of(i * chunk, chunk)
            predicted = mm(u[pl.ds(start, chunk), :], v[zz], NT)
            for kk in range(CORES):
                for yy in range(Y):
                    left = (kk * Y + yy) * block
                    p = col_of(zz, yy, kk)
                    count = counts[0, p]
                    for part in range(chunk // block):
                        b = i * (chunk // block) + part
                        found = jnp.int32(0)
                        for s in range(slots):
                            hit = (rows[s, 0, p] == b) & (count > s)
                            found = jnp.where(hit, s + 1, found)
                        live = jnp.where(found > 0, jnp.float32(1), jnp.float32(0))
                        tile = tiles[p, jnp.maximum(found - 1, 0)].astype(jnp.float32)
                        pred = predicted[part * block:(part + 1) * block, left:left + block]
                        res[pl.ds(pl.multiple_of(start + part * block, block), block), left:left + block] = (
                            (pred - tile) * live).astype(jnp.bfloat16)
            return carry

        lax.fori_loop(0, chunks, body, 0)

    def region_part(j):
        zz = zslot(j)

        def body(i, carry):
            here = pl.ds(pl.multiple_of(i * chunk, chunk), chunk)
            total = mm(res[here, :], v[zz], NN)
            if j > 0:
                total = total + racc[here, :]
            racc[here, :] = total
            if j == Z - 1:
                pltpu.make_async_copy(racc.at[here, :], region_grad.at[here, :], out_sem.at[i]).start()
            return carry

        lax.fori_loop(0, chunks, body, 0)

    def reduce_first(j):
        arrived(grecv.at[j], gc, (j,))
        gown[j] = gown[j] + grecv[j]
        for dy in range(1, Y):
            yy = lax.rem(y + dy, Y)
            for dx in range(1, R):
                s_a[j, dy - 1, (dx - 1) * n:dx * n, :] = gown[j, at_row(yy, lax.rem(x + dx, R)), :half].astype(jnp.bfloat16)
            send(s_a.at[j, dy - 1], r_a.at[j, dy - 1], ga, (j, dy), ydev(dy))
        for dx in range(1, R):
            xx = lax.rem(x + dx, R)
            for dy in range(1, Y):
                s_b[j, dx - 1, (dy - 1) * n:dy * n, :] = gown[j, at_row(lax.rem(y + dy, Y), xx), half:].astype(jnp.bfloat16)
            send(s_b.at[j, dx - 1], r_b.at[j, dx - 1], gb, (j, dx), xdev(dx))

    def reduce_second(j):
        for dy in range(1, Y):
            arrived(r_a.at[j, dy - 1], ga, (j, dy))
        for dx in range(1, R):
            here = at_row(y, lax.rem(x + dx, R))
            total = gown[j, here, :half]
            for dy in range(1, Y):
                total = total + r_a[j, dy - 1, (dx - 1) * n:dx * n, :].astype(jnp.float32)
            s_x[j, dx - 1, :, :half] = total.astype(jnp.bfloat16)
            s_x[j, dx - 1, :, half:] = gown[j, here, half:].astype(jnp.bfloat16)
            send(s_x.at[j, dx - 1], r_x.at[j, dx - 1], gx, (j, dx), xdev(dx))
        for dx in range(1, R):
            arrived(r_b.at[j, dx - 1], gb, (j, dx))
        for dy in range(1, Y):
            here = at_row(lax.rem(y + dy, Y), x)
            total = gown[j, here, half:]
            for dx in range(1, R):
                total = total + r_b[j, dx - 1, (dy - 1) * n:dy * n, :].astype(jnp.float32)
            s_y[j, dy - 1, :, half:] = total.astype(jnp.bfloat16)
            s_y[j, dy - 1, :, :half] = gown[j, here, :half].astype(jnp.bfloat16)
            send(s_y.at[j, dy - 1], r_y.at[j, dy - 1], gy, (j, dy), ydev(dy))

    def reduce_third(j):
        total = gown[j, at_row(y, x), :]
        for dx in range(1, R):
            arrived(r_x.at[j, dx - 1], gx, (j, dx))
            total = total + r_x[j, dx - 1].astype(jnp.float32)
        for dy in range(1, Y):
            arrived(r_y.at[j, dy - 1], gy, (j, dy))
            total = total + r_y[j, dy - 1].astype(jnp.float32)
        if j == 0:
            acc[...] = total
        else:
            s_z[j - 1] = total.astype(jnp.bfloat16)
            send(s_z.at[j - 1], r_z.at[j - 1], gz, (j,), zdev(j))

    def item_part(kk):
        return mm(res[:, core_rows(kk)], u[...], TN)

    def plane_next(j):
        if j < Z:
            arrived(piece(j, y, x), az, (Z - j,))
            plane_start(j)

    v[z, pl.ds(pl.multiple_of(k * side + y * block + x * n, n), n), :] = items[0]
    own = piece(0, y, x)
    plane_start(0)
    for d in range(1, Z):
        send(own, own, az, (d,), zdev(d))
    forward(0)
    plane_next(1)
    share(0)
    plane_next(2)
    shared(0)
    load_u.wait()
    load_tiles.wait()
    for j in range(Z):
        last = j == Z - 1
        residuals(j)
        if not last:
            forward(j + 1)
        if j > 0:
            reduce_second(j - 1)
        gsend[j] = item_part(1 - k)
        send(gsend.at[j], grecv.at[j], gc, (j,), sibling)
        if not last:
            share(j + 1)
        gown[j] = item_part(k)
        plane_next(j + 3)
        if not last:
            region_part(j)
        reduce_first(j)
        if j > 0:
            reduce_third(j - 1)
        if not last:
            shared(j + 1)
    region_part(Z - 1)
    reduce_second(Z - 1)
    reduce_third(Z - 1)
    total = acc[...]
    for j in range(1, Z):
        arrived(r_z.at[j - 1], gz, (j,))
        total = total + r_z[j - 1].astype(jnp.float32)
    wide = items[0].astype(jnp.float32)
    new_items[0] = wide - item_rate * (total + decay_rate * wide)
    for copy in sent:
        copy.wait_send()

    def finish(i, carry):
        here = pl.ds(pl.multiple_of(i * chunk, chunk), chunk)
        pltpu.make_async_copy(racc.at[here, :], region_grad.at[here, :], out_sem.at[i]).wait()
        return carry

    lax.fori_loop(0, chunks, finish, 0)


def on_device(R, Z, Y, region_factors, item_factors, slab_blocks, block_rows, counts):
    bf16, f32 = jnp.bfloat16, jnp.float32
    height, width = region_factors.shape
    _, panels, slots, block, _ = slab_blocks.shape
    n, half, side = block // R, width // 2, Y * block
    chunk = 4 * block
    dma = pltpu.SemaphoreType.DMA
    vmem = pltpu.VMEM
    region_grad, new_items = pl.pallas_call(
        functools.partial(kernel, R, Z, Y, chunk),
        out_shape=(jax.ShapeDtypeStruct((height, width), f32), jax.ShapeDtypeStruct(item_factors.shape, f32)),
        in_specs=[
            pl.BlockSpec(memory_space=pltpu.VMEM),
            pl.BlockSpec(memory_space=pl.ANY),
            pl.BlockSpec(memory_space=pl.ANY),
            pl.BlockSpec(memory_space=pltpu.SMEM),
            pl.BlockSpec(memory_space=pltpu.SMEM),
        ],
        out_specs=(pl.BlockSpec(memory_space=pl.ANY), pl.BlockSpec(memory_space=pltpu.VMEM)),
        scratch_shapes=[
            vmem((height, width), bf16),
            vmem((panels, slots, block, block), bf16),
            vmem((Z, CORES * side, width), bf16),
            vmem((height, CORES * side), bf16),
            vmem((height, width), f32),
            vmem((Z, side, width), f32),
            vmem((Z, side, width), f32),
            vmem((Z, side, width), f32),
            vmem((Z, Y - 1, (R - 1) * n, half), bf16),
            vmem((Z, Y - 1, (R - 1) * n, half), bf16),
            vmem((Z, R - 1, (Y - 1) * n, half), bf16),
            vmem((Z, R - 1, (Y - 1) * n, half), bf16),
            vmem((Z, R - 1, n, width), bf16),
            vmem((Z, R - 1, n, width), bf16),
            vmem((Z, Y - 1, n, width), bf16),
            vmem((Z, Y - 1, n, width), bf16),
            vmem((Z - 1, n, width), bf16),
            vmem((Z - 1, n, width), bf16),
            vmem((n, width), f32),
            dma((2,)),
            dma((height // chunk,)),
            dma((2, Z)),
            dma((2, Z, R)),
            dma((2, Z, Y)),
            dma((2, Z, R, Y)),
            dma((2, Z, R, Y)),
            dma((2, Z)),
            dma((2, Z)),
            dma((2, Z, Y)),
            dma((2, Z, R)),
            dma((2, Z, R)),
            dma((2, Z, Y)),
            dma((2, Z)),
        ],
        compiler_params=pltpu.CompilerParams(
            collective_id=0, has_side_effects=True, vmem_limit_bytes=56 * 1024 * 1024),
        cost_estimate=pl.CostEstimate(
            flops=6 * height * panels * block * width, bytes_accessed=8 * height * width, transcendentals=0),
    )(item_factors, region_factors, slab_blocks, jnp.transpose(block_rows, (2, 0, 1)), counts)
    wide = region_factors.astype(f32)
    return wide - region_rate * (region_grad + decay_rate * wide), new_items


def solution(mesh):
    R, C = mesh.shape["row"], mesh.shape["col"]
    chips = C // CORES
    Z = 4
    Y = chips // Z
    return jax.shard_map(
        functools.partial(on_device, R, Z, Y),
        mesh=mesh,
        in_specs=(
            P(("row", "col"), None),
            P("col", "row", None),
            P(("row", "col"), None, None, None, None),
            P(("row", "col"), None, None),
            P(("row", "col"), None),
        ),
        out_specs=(P(("row", "col"), None), P("col", "row", None)),
        check_vma=False,
    )
```

```python
import functools
import math

import jax
import jax.numpy as jnp
from jax import lax
from jax.experimental import pallas as pl
from jax.experimental.pallas import tpu as pltpu
from jax.sharding import PartitionSpec as P

region_rate = 0.05
item_rate = 0.01
decay_rate = 0.1

MESH = pl.DeviceIdType.MESH
CORES = 2
NT = (((1,), (1,)), ((), ()))
TN = (((0,), (0,)), ((), ()))
NN = (((1,), (0,)), ((), ()))


def mm(a, b, dims):
    return lax.dot_general(a, b, dims, preferred_element_type=jnp.float32)


def kernel(R, Z, Y, chunk, items, regions, slab, rows, counts, region_grad, new_items,
           u, tiles, v, res, racc, gown, gsend, grecv,
           s_a, r_a, s_b, r_b, s_x, r_x, s_y, r_y, s_z, r_z, acc,
           loc_sem, out_sem, az, ax, ay, aa, ab, sib, gc, ga, gb, gx, gy, gz):
    x = lax.axis_index("row")
    c = lax.axis_index("col")
    k = lax.rem(c, CORES)
    y = lax.rem(c // CORES, Y)
    z = c // (CORES * Y)
    block = tiles.shape[-1]
    width = u.shape[-1]
    half = width // 2
    n = block // R
    slots = tiles.shape[1]
    chunks = u.shape[0] // chunk

    def col_of(zz, yy, kk):
        return (zz * Y + yy) * CORES + kk

    def xdev(d):
        return {"row": lax.rem(x + d, R), "col": c}

    def ydev(d):
        return {"row": x, "col": col_of(z, lax.rem(y + d, Y), k)}

    def zdev(d):
        return {"row": x, "col": col_of(lax.rem(z + d, Z), y, k)}

    sibling = {"row": x, "col": col_of(z, y, 1 - k)}
    peers = [xdev(d) for d in range(1, R)] + [ydev(d) for d in range(1, Y)] + [zdev(d) for d in range(1, Z)] + [sibling]

    load_u = pltpu.make_async_copy(regions, u, loc_sem.at[0])
    load_u.start()
    load_tiles = pltpu.make_async_copy(slab.at[0], tiles, loc_sem.at[1])
    load_tiles.start()

    barrier = pltpu.get_barrier_semaphore()
    for peer in peers:
        pl.semaphore_signal(barrier, inc=1, device_id=peer, device_id_type=MESH)
    pl.semaphore_wait(barrier, len(peers))

    sent = []

    def remote(src, dst, sems, index, device):
        return pltpu.make_async_remote_copy(
            src_ref=src, dst_ref=dst, send_sem=sems.at[(0,) + index], recv_sem=sems.at[(1,) + index],
            device_id=device, device_id_type=MESH)

    def send(src, dst, sems, index, device):
        copy = remote(src, dst, sems, index, device)
        copy.start()
        sent.append(copy)

    def arrived(dst, sems, index):
        remote(dst, dst, sems, index, sibling).wait_recv()

    def zslot(j):
        return lax.rem(z + j, Z)

    def xback(d):
        return lax.rem(x + R - d, R)

    def yback(d):
        return lax.rem(y + Y - d, Y)

    side = Y * block

    def at_row(yy, xx):
        return pl.ds(pl.multiple_of(yy * block + xx * n, n), n)

    def core_rows(kk):
        return pl.ds(pl.multiple_of(kk * side, side), side)

    def piece(j, yy, xx, columns=slice(None)):
        return v.at[zslot(j), pl.ds(pl.multiple_of(k * side + yy * block + xx * n, n), n), columns]

    first, second = pl.ds(0, half), pl.ds(half, half)

    def plane_start(j):
        own = piece(j, y, x)
        for d in range(1, R):
            send(own, own, ax, (j, d), xdev(d))
        for d in range(1, Y):
            send(own, own, ay, (j, d), ydev(d))

    def forward(j):
        for dx in range(1, R):
            arrived(piece(j, y, xback(dx)), ax, (j, dx))
            part = piece(j, y, xback(dx), first)
            for dy in range(1, Y):
                send(part, part, aa, (j, dx, dy), ydev(dy))
        for dy in range(1, Y):
            arrived(piece(j, yback(dy), x), ay, (j, dy))
            part = piece(j, yback(dy), x, second)
            for dx in range(1, R):
                send(part, part, ab, (j, dx, dy), xdev(dx))

    def share(j):
        for dx in range(1, R):
            for dy in range(1, Y):
                arrived(piece(j, yback(dy), xback(dx), first), aa, (j, dx, dy))
                arrived(piece(j, yback(dy), xback(dx), second), ab, (j, dx, dy))
        mine = v.at[zslot(j), core_rows(k)]
        send(mine, mine, sib, (j,), sibling)

    def shared(j):
        arrived(v.at[zslot(j), core_rows(1 - k)], sib, (j,))

    def residuals(j):
        zz = zslot(j)

        def body(i, carry):
            start = pl.multiple_of(i * chunk, chunk)
            predicted = mm(u[pl.ds(start, chunk), :], v[zz], NT)
            for kk in range(CORES):
                for yy in range(Y):
                    left = (kk * Y + yy) * block
                    p = col_of(zz, yy, kk)
                    count = counts[0, p]
                    for part in range(chunk // block):
                        b = i * (chunk // block) + part
                        found = jnp.int32(0)
                        for s in range(slots):
                            hit = (rows[s, 0, p] == b) & (count > s)
                            found = jnp.where(hit, s + 1, found)
                        live = jnp.where(found > 0, jnp.float32(1), jnp.float32(0))
                        tile = tiles[p, jnp.maximum(found - 1, 0)].astype(jnp.float32)
                        pred = predicted[part * block:(part + 1) * block, left:left + block]
                        res[pl.ds(pl.multiple_of(start + part * block, block), block), left:left + block] = (
                            (pred - tile) * live).astype(jnp.bfloat16)
            return carry

        lax.fori_loop(0, chunks, body, 0)

    def region_part(j):
        zz = zslot(j)

        def body(i, carry):
            here = pl.ds(pl.multiple_of(i * chunk, chunk), chunk)
            total = mm(res[here, :], v[zz], NN)
            if j > 0:
                total = total + racc[here, :]
            racc[here, :] = total
            if j == Z - 1:
                pltpu.make_async_copy(racc.at[here, :], region_grad.at[here, :], out_sem.at[i]).start()
            return carry

        lax.fori_loop(0, chunks, body, 0)

    def reduce_first(j):
        arrived(grecv.at[j], gc, (j,))
        gown[j] = gown[j] + grecv[j]
        for dy in range(1, Y):
            yy = lax.rem(y + dy, Y)
            for dx in range(1, R):
                s_a[j, dy - 1, (dx - 1) * n:dx * n, :] = gown[j, at_row(yy, lax.rem(x + dx, R)), :half].astype(jnp.bfloat16)
            send(s_a.at[j, dy - 1], r_a.at[j, dy - 1], ga, (j, dy), ydev(dy))
        for dx in range(1, R):
            xx = lax.rem(x + dx, R)
            for dy in range(1, Y):
                s_b[j, dx - 1, (dy - 1) * n:dy * n, :] = gown[j, at_row(lax.rem(y + dy, Y), xx), half:].astype(jnp.bfloat16)
            send(s_b.at[j, dx - 1], r_b.at[j, dx - 1], gb, (j, dx), xdev(dx))

    def reduce_second(j):
        for dy in range(1, Y):
            arrived(r_a.at[j, dy - 1], ga, (j, dy))
        for dx in range(1, R):
            here = at_row(y, lax.rem(x + dx, R))
            total = gown[j, here, :half]
            for dy in range(1, Y):
                total = total + r_a[j, dy - 1, (dx - 1) * n:dx * n, :].astype(jnp.float32)
            s_x[j, dx - 1, :, :half] = total.astype(jnp.bfloat16)
            s_x[j, dx - 1, :, half:] = gown[j, here, half:].astype(jnp.bfloat16)
            send(s_x.at[j, dx - 1], r_x.at[j, dx - 1], gx, (j, dx), xdev(dx))
        for dx in range(1, R):
            arrived(r_b.at[j, dx - 1], gb, (j, dx))
        for dy in range(1, Y):
            here = at_row(lax.rem(y + dy, Y), x)
            total = gown[j, here, half:]
            for dx in range(1, R):
                total = total + r_b[j, dx - 1, (dy - 1) * n:dy * n, :].astype(jnp.float32)
            s_y[j, dy - 1, :, half:] = total.astype(jnp.bfloat16)
            s_y[j, dy - 1, :, :half] = gown[j, here, :half].astype(jnp.bfloat16)
            send(s_y.at[j, dy - 1], r_y.at[j, dy - 1], gy, (j, dy), ydev(dy))

    def reduce_third(j):
        total = gown[j, at_row(y, x), :]
        for dx in range(1, R):
            arrived(r_x.at[j, dx - 1], gx, (j, dx))
            total = total + r_x[j, dx - 1].astype(jnp.float32)
        for dy in range(1, Y):
            arrived(r_y.at[j, dy - 1], gy, (j, dy))
            total = total + r_y[j, dy - 1].astype(jnp.float32)
        if j == 0:
            acc[...] = total
        else:
            s_z[j - 1] = total.astype(jnp.bfloat16)
            send(s_z.at[j - 1], r_z.at[j - 1], gz, (j,), zdev(j))

    def item_part(kk):
        return mm(res[:, core_rows(kk)], u[...], TN)

    def plane_next(j):
        if j < Z:
            arrived(piece(j, y, x), az, (Z - j,))
            plane_start(j)

    v[z, pl.ds(pl.multiple_of(k * side + y * block + x * n, n), n), :] = items[0]
    own = piece(0, y, x)
    plane_start(0)
    for d in range(1, Z):
        send(own, own, az, (d,), zdev(d))
    forward(0)
    plane_next(1)
    share(0)
    plane_next(2)
    forward(1)
    shared(0)
    plane_next(3)
    load_u.wait()
    load_tiles.wait()
    for j in range(Z):
        last = j == Z - 1
        residuals(j)
        if not last:
            share(j + 1)
        if j + 2 < Z:
            forward(j + 2)
        if j > 0:
            reduce_first(j - 1)
        gsend[j] = item_part(1 - k)
        send(gsend.at[j], grecv.at[j], gc, (j,), sibling)
        if j > 1:
            reduce_third(j - 2)
        gown[j] = item_part(k)
        if not last:
            region_part(j)
            if j > 0:
                reduce_second(j - 1)
            shared(j + 1)
    reduce_first(Z - 1)
    reduce_second(Z - 2)
    region_part(Z - 1)
    reduce_second(Z - 1)
    reduce_third(Z - 2)
    reduce_third(Z - 1)
    total = acc[...]
    for j in range(1, Z):
        arrived(r_z.at[j - 1], gz, (j,))
        total = total + r_z[j - 1].astype(jnp.float32)
    wide = items[0].astype(jnp.float32)
    new_items[0] = wide - item_rate * (total + decay_rate * wide)
    for copy in sent:
        copy.wait_send()

    def finish(i, carry):
        here = pl.ds(pl.multiple_of(i * chunk, chunk), chunk)
        pltpu.make_async_copy(racc.at[here, :], region_grad.at[here, :], out_sem.at[i]).wait()
        return carry

    lax.fori_loop(0, chunks, finish, 0)


def on_device(R, Z, Y, region_factors, item_factors, slab_blocks, block_rows, counts):
    bf16, f32 = jnp.bfloat16, jnp.float32
    height, width = region_factors.shape
    _, panels, slots, block, _ = slab_blocks.shape
    n, half, side = block // R, width // 2, Y * block
    chunk = 4 * block
    dma = pltpu.SemaphoreType.DMA
    vmem = pltpu.VMEM
    buffers = [
        vmem((height, width), bf16),
        vmem((panels, slots, block, block), bf16),
        vmem((Z, CORES * side, width), bf16),
        vmem((height, CORES * side), bf16),
        vmem((height, width), f32),
        vmem((Z, side, width), f32),
        vmem((Z, side, width), f32),
        vmem((Z, side, width), f32),
        vmem((Z, Y - 1, (R - 1) * n, half), bf16),
        vmem((Z, Y - 1, (R - 1) * n, half), bf16),
        vmem((Z, R - 1, (Y - 1) * n, half), bf16),
        vmem((Z, R - 1, (Y - 1) * n, half), bf16),
        vmem((Z, R - 1, n, width), bf16),
        vmem((Z, R - 1, n, width), bf16),
        vmem((Z, Y - 1, n, width), bf16),
        vmem((Z, Y - 1, n, width), bf16),
        vmem((Z - 1, n, width), bf16),
        vmem((Z - 1, n, width), bf16),
        vmem((n, width), f32),
    ]
    semaphores = [
        dma((2,)),
        dma((height // chunk,)),
        dma((2, Z)),
        dma((2, Z, R)),
        dma((2, Z, Y)),
        dma((2, Z, R, Y)),
        dma((2, Z, R, Y)),
        dma((2, Z)),
        dma((2, Z)),
        dma((2, Z, Y)),
        dma((2, Z, R)),
        dma((2, Z, R)),
        dma((2, Z, Y)),
        dma((2, Z)),
    ]
    held = sum(math.prod(buffer.shape) * jnp.dtype(buffer.dtype).itemsize for buffer in buffers)
    region_grad, new_items = pl.pallas_call(
        functools.partial(kernel, R, Z, Y, chunk),
        out_shape=(jax.ShapeDtypeStruct((height, width), f32), jax.ShapeDtypeStruct(item_factors.shape, f32)),
        in_specs=[
            pl.BlockSpec(memory_space=pltpu.VMEM),
            pl.BlockSpec(memory_space=pltpu.HBM),
            pl.BlockSpec(memory_space=pltpu.HBM),
            pl.BlockSpec(memory_space=pltpu.SMEM),
            pl.BlockSpec(memory_space=pltpu.SMEM),
        ],
        out_specs=(pl.BlockSpec(memory_space=pl.ANY), pl.BlockSpec(memory_space=pltpu.VMEM)),
        scratch_shapes=buffers + semaphores,
        compiler_params=pltpu.CompilerParams(
            collective_id=0, has_side_effects=True, vmem_limit_bytes=held + 8 * 1024 * 1024),
        cost_estimate=pl.CostEstimate(
            flops=6 * height * panels * block * width, bytes_accessed=8 * height * width, transcendentals=0),
    )(item_factors, region_factors, slab_blocks, jnp.transpose(block_rows, (2, 0, 1)), counts)
    wide = region_factors.astype(f32)
    return wide - region_rate * (region_grad + decay_rate * wide), new_items


def solution(mesh):
    R, C = mesh.shape["row"], mesh.shape["col"]
    chips = C // CORES
    Z = 4
    Y = chips // Z
    return jax.shard_map(
        functools.partial(on_device, R, Z, Y),
        mesh=mesh,
        in_specs=(
            P(("row", "col"), None),
            P("col", "row", None),
            P(("row", "col"), None, None, None, None),
            P(("row", "col"), None, None),
            P(("row", "col"), None),
        ),
        out_specs=(P(("row", "col"), None), P("col", "row", None)),
        check_vma=False,
    )
```

```python
import functools

import jax
import jax.numpy as jnp
from jax import lax
from jax.experimental import pallas as pl
from jax.experimental.pallas import tpu as pltpu
from jax.sharding import PartitionSpec as P

region_rate = 0.05
item_rate = 0.01
decay_rate = 0.1

MESH = pl.DeviceIdType.MESH
CORES = 2
NT = (((1,), (1,)), ((), ()))
NN = (((1,), (0,)), ((), ()))


def mm(a, b, dims):
    return lax.dot_general(a, b, dims, preferred_element_type=jnp.float32)


def kernel(R, Z, Y, chunk, items, regions, slab, rows, counts, region_grad, new_items,
           u, tiles, v, res, ut, gkept, gown, gsend, grecv,
           s_a, r_a, s_b, r_b, s_x, r_x, s_y, r_y, s_z, r_z, acc,
           loc_sem, az, ax, ay, aa, ab, sib, gc, ga, gb, gx, gy, gz):
    x = lax.axis_index("row")
    c = lax.axis_index("col")
    k = lax.rem(c, CORES)
    y = lax.rem(c // CORES, Y)
    z = c // (CORES * Y)
    block = tiles.shape[-1]
    width = u.shape[-1]
    half = width // 2
    n = block // R
    slots = tiles.shape[1]

    def col_of(zz, yy, kk):
        return (zz * Y + yy) * CORES + kk

    def xdev(d):
        return {"row": lax.rem(x + d, R), "col": c}

    def ydev(d):
        return {"row": x, "col": col_of(z, lax.rem(y + d, Y), k)}

    def zdev(d):
        return {"row": x, "col": col_of(lax.rem(z + d, Z), y, k)}

    sibling = {"row": x, "col": col_of(z, y, 1 - k)}
    peers = [xdev(d) for d in range(1, R)] + [ydev(d) for d in range(1, Y)] + [zdev(d) for d in range(1, Z)] + [sibling]

    load_u = pltpu.make_async_copy(regions, u, loc_sem.at[0])
    load_u.start()
    load_tiles = pltpu.make_async_copy(slab.at[0], tiles, loc_sem.at[1])
    load_tiles.start()

    barrier = pltpu.get_barrier_semaphore()
    for peer in peers:
        pl.semaphore_signal(barrier, inc=1, device_id=peer, device_id_type=MESH)
    pl.semaphore_wait(barrier, len(peers))

    sent = []

    def remote(src, dst, sems, index, device):
        return pltpu.make_async_remote_copy(
            src_ref=src, dst_ref=dst, send_sem=sems.at[(0,) + index], recv_sem=sems.at[(1,) + index],
            device_id=device, device_id_type=MESH)

    def send(src, dst, sems, index, device):
        copy = remote(src, dst, sems, index, device)
        copy.start()
        sent.append(copy)

    def arrived(dst, sems, index):
        remote(dst, dst, sems, index, sibling).wait_recv()

    def zslot(j):
        return lax.rem(z + j, Z)

    def xback(d):
        return lax.rem(x + R - d, R)

    def yback(d):
        return lax.rem(y + Y - d, Y)

    side = Y * block

    def at_row(yy, xx):
        return pl.ds(pl.multiple_of(yy * block + xx * n, n), n)

    def core_rows(kk):
        return pl.ds(pl.multiple_of(kk * side, side), side)

    def piece(j, yy, xx, columns=slice(None)):
        return v.at[zslot(j), pl.ds(pl.multiple_of(k * side + yy * block + xx * n, n), n), columns]

    first, second = pl.ds(0, half), pl.ds(half, half)

    def plane_start(j):
        own = piece(j, y, x)
        for d in range(1, R):
            send(own, own, ax, (j, d), xdev(d))
        for d in range(1, Y):
            send(own, own, ay, (j, d), ydev(d))

    def forward(j):
        for dx in range(1, R):
            arrived(piece(j, y, xback(dx)), ax, (j, dx))
            part = piece(j, y, xback(dx), first)
            for dy in range(1, Y):
                send(part, part, aa, (j, dx, dy), ydev(dy))
        for dy in range(1, Y):
            arrived(piece(j, yback(dy), x), ay, (j, dy))
            part = piece(j, yback(dy), x, second)
            for dx in range(1, R):
                send(part, part, ab, (j, dx, dy), xdev(dx))

    def share(j):
        for dx in range(1, R):
            for dy in range(1, Y):
                arrived(piece(j, yback(dy), xback(dx), first), aa, (j, dx, dy))
                arrived(piece(j, yback(dy), xback(dx), second), ab, (j, dx, dy))
        mine = v.at[zslot(j), core_rows(k)]
        send(mine, mine, sib, (j,), sibling)

    def shared(j):
        arrived(v.at[zslot(j), core_rows(1 - k)], sib, (j,))

    def residuals(j):
        zz = zslot(j)

        def body(i, carry):
            start = pl.multiple_of(i * chunk, chunk)
            predicted = mm(u[pl.ds(start, chunk), :], v[zz], NT)
            for kk in range(CORES):
                for yy in range(Y):
                    left = (kk * Y + yy) * block
                    p = col_of(zz, yy, kk)
                    count = counts[0, p]
                    for part in range(chunk // block):
                        b = i * (chunk // block) + part
                        found = jnp.int32(0)
                        for s in range(slots):
                            hit = (rows[s, 0, p] == b) & (count > s)
                            found = jnp.where(hit, s + 1, found)
                        live = jnp.where(found > 0, jnp.float32(1), jnp.float32(0))
                        tile = tiles[p, jnp.maximum(found - 1, 0)].astype(jnp.float32)
                        pred = predicted[part * block:(part + 1) * block, left:left + block]
                        res[pl.ds(pl.multiple_of(start + part * block, block), block), left:left + block] = (
                            (pred - tile) * live).astype(jnp.bfloat16)
            return carry

        lax.fori_loop(0, u.shape[0] // chunk, body, 0)

    def region_part(j):
        zz = zslot(j)

        def body(i, carry):
            here = pl.ds(pl.multiple_of(i * chunk, chunk), chunk)
            total = mm(res[here, :], v[zz], NN)
            if j > 0:
                total = total + region_grad[here, :]
            region_grad[here, :] = total
            return carry

        lax.fori_loop(0, u.shape[0] // chunk, body, 0)

    def reduce_first(j):
        arrived(grecv.at[j], gc, (j,))
        gown[j] = jnp.transpose(gkept[j] + grecv[j])
        for dy in range(1, Y):
            yy = lax.rem(y + dy, Y)
            for dx in range(1, R):
                s_a[j, dy - 1, (dx - 1) * n:dx * n, :] = gown[j, at_row(yy, lax.rem(x + dx, R)), :half].astype(jnp.bfloat16)
            send(s_a.at[j, dy - 1], r_a.at[j, dy - 1], ga, (j, dy), ydev(dy))
        for dx in range(1, R):
            xx = lax.rem(x + dx, R)
            for dy in range(1, Y):
                s_b[j, dx - 1, (dy - 1) * n:dy * n, :] = gown[j, at_row(lax.rem(y + dy, Y), xx), half:].astype(jnp.bfloat16)
            send(s_b.at[j, dx - 1], r_b.at[j, dx - 1], gb, (j, dx), xdev(dx))

    def reduce_second(j):
        for dy in range(1, Y):
            arrived(r_a.at[j, dy - 1], ga, (j, dy))
        for dx in range(1, R):
            here = at_row(y, lax.rem(x + dx, R))
            total = gown[j, here, :half]
            for dy in range(1, Y):
                total = total + r_a[j, dy - 1, (dx - 1) * n:dx * n, :].astype(jnp.float32)
            s_x[j, dx - 1, :, :half] = total.astype(jnp.bfloat16)
            s_x[j, dx - 1, :, half:] = gown[j, here, half:].astype(jnp.bfloat16)
            send(s_x.at[j, dx - 1], r_x.at[j, dx - 1], gx, (j, dx), xdev(dx))
        for dx in range(1, R):
            arrived(r_b.at[j, dx - 1], gb, (j, dx))
        for dy in range(1, Y):
            here = at_row(lax.rem(y + dy, Y), x)
            total = gown[j, here, half:]
            for dx in range(1, R):
                total = total + r_b[j, dx - 1, (dy - 1) * n:dy * n, :].astype(jnp.float32)
            s_y[j, dy - 1, :, half:] = total.astype(jnp.bfloat16)
            s_y[j, dy - 1, :, :half] = gown[j, here, :half].astype(jnp.bfloat16)
            send(s_y.at[j, dy - 1], r_y.at[j, dy - 1], gy, (j, dy), ydev(dy))

    def reduce_third(j):
        total = gown[j, at_row(y, x), :]
        for dx in range(1, R):
            arrived(r_x.at[j, dx - 1], gx, (j, dx))
            total = total + r_x[j, dx - 1].astype(jnp.float32)
        for dy in range(1, Y):
            arrived(r_y.at[j, dy - 1], gy, (j, dy))
            total = total + r_y[j, dy - 1].astype(jnp.float32)
        if j == 0:
            acc[...] = total
        else:
            s_z[j - 1] = total.astype(jnp.bfloat16)
            send(s_z.at[j - 1], r_z.at[j - 1], gz, (j,), zdev(j))

    def item_part(kk):
        return mm(ut[...], res[:, core_rows(kk)], NN)

    def plane_next(j):
        if j < Z:
            arrived(piece(j, y, x), az, (Z - j,))
            plane_start(j)

    v[z, pl.ds(pl.multiple_of(k * side + y * block + x * n, n), n), :] = items[0]
    own = piece(0, y, x)
    plane_start(0)
    for d in range(1, Z):
        send(own, own, az, (d,), zdev(d))
    forward(0)
    plane_next(1)
    load_u.wait()
    ut[...] = jnp.transpose(u[...])
    share(0)
    plane_next(2)
    forward(1)
    shared(0)
    plane_next(3)
    load_tiles.wait()
    for j in range(Z):
        last = j == Z - 1
        residuals(j)
        if not last:
            share(j + 1)
        if j + 2 < Z:
            forward(j + 2)
        if j > 0:
            reduce_first(j - 1)
        gsend[j] = item_part(1 - k)
        send(gsend.at[j], grecv.at[j], gc, (j,), sibling)
        if j > 1:
            reduce_third(j - 2)
        gkept[j] = item_part(k)
        if not last:
            region_part(j)
            if j > 0:
                reduce_second(j - 1)
            shared(j + 1)
    reduce_first(Z - 1)
    reduce_second(Z - 2)
    region_part(Z - 1)
    reduce_second(Z - 1)
    reduce_third(Z - 2)
    reduce_third(Z - 1)
    total = acc[...]
    for j in range(1, Z):
        arrived(r_z.at[j - 1], gz, (j,))
        total = total + r_z[j - 1].astype(jnp.float32)
    wide = items[0].astype(jnp.float32)
    new_items[0] = wide - item_rate * (total + decay_rate * wide)
    for copy in sent:
        copy.wait_send()


def on_device(R, Z, Y, region_factors, item_factors, slab_blocks, block_rows, counts):
    bf16, f32 = jnp.bfloat16, jnp.float32
    height, width = region_factors.shape
    _, panels, slots, block, _ = slab_blocks.shape
    n, half, side = block // R, width // 2, Y * block
    chunk = height
    dma = pltpu.SemaphoreType.DMA
    vmem = pltpu.VMEM
    buffers = [
        vmem((height, width), bf16),
        vmem((panels, slots, block, block), bf16),
        vmem((Z, CORES * side, width), bf16),
        vmem((height, CORES * side), bf16),
        vmem((width, height), bf16),
        vmem((Z, width, side), f32),
        vmem((Z, side, width), f32),
        vmem((Z, width, side), f32),
        vmem((Z, width, side), f32),
        vmem((Z, Y - 1, (R - 1) * n, half), bf16),
        vmem((Z, Y - 1, (R - 1) * n, half), bf16),
        vmem((Z, R - 1, (Y - 1) * n, half), bf16),
        vmem((Z, R - 1, (Y - 1) * n, half), bf16),
        vmem((Z, R - 1, n, width), bf16),
        vmem((Z, R - 1, n, width), bf16),
        vmem((Z, Y - 1, n, width), bf16),
        vmem((Z, Y - 1, n, width), bf16),
        vmem((Z - 1, n, width), bf16),
        vmem((Z - 1, n, width), bf16),
        vmem((n, width), f32),
    ]
    semaphores = [
        dma((2,)),
        dma((2, Z)),
        dma((2, Z, R)),
        dma((2, Z, Y)),
        dma((2, Z, R, Y)),
        dma((2, Z, R, Y)),
        dma((2, Z)),
        dma((2, Z)),
        dma((2, Z, Y)),
        dma((2, Z, R)),
        dma((2, Z, R)),
        dma((2, Z, Y)),
        dma((2, Z)),
    ]
    region_grad, new_items = pl.pallas_call(
        functools.partial(kernel, R, Z, Y, chunk),
        out_shape=(pltpu.VMEM((height, width), f32), pltpu.VMEM(item_factors.shape, f32)),
        in_specs=[
            pl.BlockSpec(memory_space=pltpu.VMEM),
            pl.BlockSpec(memory_space=pltpu.HBM),
            pl.BlockSpec(memory_space=pltpu.HBM),
            pl.BlockSpec(memory_space=pltpu.SMEM),
            pl.BlockSpec(memory_space=pltpu.SMEM),
        ],
        out_specs=(pl.BlockSpec(memory_space=pltpu.VMEM), pl.BlockSpec(memory_space=pltpu.VMEM)),
        scratch_shapes=buffers + semaphores,
        compiler_params=pltpu.CompilerParams(
            collective_id=0, has_side_effects=True, vmem_limit_bytes=56 * 1024 * 1024),
        cost_estimate=pl.CostEstimate(
            flops=6 * height * panels * block * width, bytes_accessed=8 * height * width, transcendentals=0),
    )(item_factors, region_factors, slab_blocks, jnp.transpose(block_rows, (2, 0, 1)), counts)
    wide = region_factors.astype(f32)
    return wide - region_rate * (region_grad + decay_rate * wide), new_items


def solution(mesh):
    R, C = mesh.shape["row"], mesh.shape["col"]
    chips = C // CORES
    Z = 4
    Y = chips // Z
    return jax.shard_map(
        functools.partial(on_device, R, Z, Y),
        mesh=mesh,
        in_specs=(
            P(("row", "col"), None),
            P("col", "row", None),
            P(("row", "col"), None, None, None, None),
            P(("row", "col"), None, None),
            P(("row", "col"), None),
        ),
        out_specs=(P(("row", "col"), None), P("col", "row", None)),
        check_vma=False,
    )
```

```python
import functools

import jax
import jax.numpy as jnp
from jax import lax
from jax.experimental import pallas as pl
from jax.experimental.pallas import tpu as pltpu
from jax.sharding import PartitionSpec as P

region_rate = 0.05
item_rate = 0.01
decay_rate = 0.1

MESH = pl.DeviceIdType.MESH
CORES = 2
NT = (((1,), (1,)), ((), ()))
NN = (((1,), (0,)), ((), ()))


def mm(a, b, dims):
    return lax.dot_general(a, b, dims, preferred_element_type=jnp.float32)


def kernel(R, Z, Y, chunk, items, regions, slab, rows, counts, region_grad, new_items,
           u, tiles, v, res, ut, gkept, gown, gsend, grecv,
           s_a, r_a, s_b, r_b, s_x, r_x, s_y, r_y, s_z, r_z, acc,
           loc_sem, az, ax, ay, aa, ab, sib, gc, ga, gb, gx, gy, gz):
    x = lax.axis_index("row")
    c = lax.axis_index("col")
    k = lax.rem(c, CORES)
    y = lax.rem(c // CORES, Y)
    z = c // (CORES * Y)
    block = tiles.shape[-1]
    width = u.shape[-1]
    half = width // 2
    n = block // R
    slots = tiles.shape[1]

    def col_of(zz, yy, kk):
        return (zz * Y + yy) * CORES + kk

    def xdev(d):
        return {"row": lax.rem(x + d, R), "col": c}

    def ydev(d):
        return {"row": x, "col": col_of(z, lax.rem(y + d, Y), k)}

    def zdev(d):
        return {"row": x, "col": col_of(lax.rem(z + d, Z), y, k)}

    sibling = {"row": x, "col": col_of(z, y, 1 - k)}
    peers = [xdev(d) for d in range(1, R)] + [ydev(d) for d in range(1, Y)] + [zdev(d) for d in range(1, Z)] + [sibling]

    load_u = pltpu.make_async_copy(regions, u, loc_sem.at[0])
    load_u.start()
    load_tiles = pltpu.make_async_copy(slab.at[0], tiles, loc_sem.at[1])
    load_tiles.start()

    barrier = pltpu.get_barrier_semaphore()
    for peer in peers:
        pl.semaphore_signal(barrier, inc=1, device_id=peer, device_id_type=MESH)
    pl.semaphore_wait(barrier, len(peers))

    sent = []

    def remote(src, dst, sems, index, device):
        return pltpu.make_async_remote_copy(
            src_ref=src, dst_ref=dst, send_sem=sems.at[(0,) + index], recv_sem=sems.at[(1,) + index],
            device_id=device, device_id_type=MESH)

    def send(src, dst, sems, index, device):
        copy = remote(src, dst, sems, index, device)
        copy.start()
        sent.append(copy)

    def arrived(dst, sems, index):
        remote(dst, dst, sems, index, sibling).wait_recv()

    def zslot(j):
        return lax.rem(z + j, Z)

    def xback(d):
        return lax.rem(x + R - d, R)

    def yback(d):
        return lax.rem(y + Y - d, Y)

    side = Y * block

    def at_row(yy, xx):
        return pl.ds(pl.multiple_of(yy * block + xx * n, n), n)

    def core_rows(kk):
        return pl.ds(pl.multiple_of(kk * side, side), side)

    def piece(j, yy, xx, columns=slice(None)):
        return v.at[zslot(j), pl.ds(pl.multiple_of(k * side + yy * block + xx * n, n), n), columns]

    first, second = pl.ds(0, half), pl.ds(half, half)

    def plane_start(j):
        own = piece(j, y, x)
        for d in range(1, R):
            send(own, own, ax, (j, d), xdev(d))
        for d in range(1, Y):
            send(own, own, ay, (j, d), ydev(d))

    def forward(j):
        for dx in range(1, R):
            arrived(piece(j, y, xback(dx)), ax, (j, dx))
            part = piece(j, y, xback(dx), first)
            for dy in range(1, Y):
                send(part, part, aa, (j, dx, dy), ydev(dy))
        for dy in range(1, Y):
            arrived(piece(j, yback(dy), x), ay, (j, dy))
            part = piece(j, yback(dy), x, second)
            for dx in range(1, R):
                send(part, part, ab, (j, dx, dy), xdev(dx))

    def share(j):
        for dx in range(1, R):
            for dy in range(1, Y):
                arrived(piece(j, yback(dy), xback(dx), first), aa, (j, dx, dy))
                arrived(piece(j, yback(dy), xback(dx), second), ab, (j, dx, dy))
        mine = v.at[zslot(j), core_rows(k)]
        send(mine, mine, sib, (j,), sibling)

    def shared(j):
        arrived(v.at[zslot(j), core_rows(1 - k)], sib, (j,))

    def residuals(j):
        zz = zslot(j)

        def body(i, carry):
            start = pl.multiple_of(i * chunk, chunk)
            predicted = mm(u[pl.ds(start, chunk), :], v[zz], NT)
            for kk in range(CORES):
                for yy in range(Y):
                    left = (kk * Y + yy) * block
                    p = col_of(zz, yy, kk)
                    count = counts[0, p]
                    for part in range(chunk // block):
                        b = i * (chunk // block) + part
                        found = jnp.int32(0)
                        for s in range(slots):
                            hit = (rows[s, 0, p] == b) & (count > s)
                            found = jnp.where(hit, s + 1, found)
                        live = jnp.where(found > 0, jnp.float32(1), jnp.float32(0))
                        tile = tiles[p, jnp.maximum(found - 1, 0)].astype(jnp.float32)
                        pred = predicted[part * block:(part + 1) * block, left:left + block]
                        res[pl.ds(pl.multiple_of(start + part * block, block), block), left:left + block] = (
                            (pred - tile) * live).astype(jnp.bfloat16)
            return carry

        lax.fori_loop(0, u.shape[0] // chunk, body, 0)

    def region_part(j):
        zz = zslot(j)

        def body(i, carry):
            here = pl.ds(pl.multiple_of(i * chunk, chunk), chunk)
            total = mm(res[here, :], v[zz], NN)
            if j > 0:
                total = total + region_grad[here, :]
            region_grad[here, :] = total
            return carry

        lax.fori_loop(0, u.shape[0] // chunk, body, 0)

    def reduce_first(j):
        arrived(grecv.at[j], gc, (j,))
        gown[j] = jnp.transpose(gkept[j] + grecv[j].astype(jnp.float32))
        for dy in range(1, Y):
            yy = lax.rem(y + dy, Y)
            for dx in range(1, R):
                s_a[j, dy - 1, (dx - 1) * n:dx * n, :] = gown[j, at_row(yy, lax.rem(x + dx, R)), :half].astype(jnp.bfloat16)
            send(s_a.at[j, dy - 1], r_a.at[j, dy - 1], ga, (j, dy), ydev(dy))
        for dx in range(1, R):
            xx = lax.rem(x + dx, R)
            for dy in range(1, Y):
                s_b[j, dx - 1, (dy - 1) * n:dy * n, :] = gown[j, at_row(lax.rem(y + dy, Y), xx), half:].astype(jnp.bfloat16)
            send(s_b.at[j, dx - 1], r_b.at[j, dx - 1], gb, (j, dx), xdev(dx))

    def reduce_second(j):
        for dy in range(1, Y):
            arrived(r_a.at[j, dy - 1], ga, (j, dy))
        for dx in range(1, R):
            here = at_row(y, lax.rem(x + dx, R))
            total = gown[j, here, :half]
            for dy in range(1, Y):
                total = total + r_a[j, dy - 1, (dx - 1) * n:dx * n, :].astype(jnp.float32)
            s_x[j, dx - 1, :, :half] = total.astype(jnp.bfloat16)
            s_x[j, dx - 1, :, half:] = gown[j, here, half:].astype(jnp.bfloat16)
            send(s_x.at[j, dx - 1], r_x.at[j, dx - 1], gx, (j, dx), xdev(dx))
        for dx in range(1, R):
            arrived(r_b.at[j, dx - 1], gb, (j, dx))
        for dy in range(1, Y):
            here = at_row(lax.rem(y + dy, Y), x)
            total = gown[j, here, half:]
            for dx in range(1, R):
                total = total + r_b[j, dx - 1, (dy - 1) * n:dy * n, :].astype(jnp.float32)
            s_y[j, dy - 1, :, half:] = total.astype(jnp.bfloat16)
            s_y[j, dy - 1, :, :half] = gown[j, here, :half].astype(jnp.bfloat16)
            send(s_y.at[j, dy - 1], r_y.at[j, dy - 1], gy, (j, dy), ydev(dy))

    def reduce_third(j):
        total = gown[j, at_row(y, x), :]
        for dx in range(1, R):
            arrived(r_x.at[j, dx - 1], gx, (j, dx))
            total = total + r_x[j, dx - 1].astype(jnp.float32)
        for dy in range(1, Y):
            arrived(r_y.at[j, dy - 1], gy, (j, dy))
            total = total + r_y[j, dy - 1].astype(jnp.float32)
        if j == 0:
            acc[...] = total
        else:
            s_z[j - 1] = total.astype(jnp.bfloat16)
            send(s_z.at[j - 1], r_z.at[j - 1], gz, (j,), zdev(j))

    def item_part(kk):
        return mm(ut[...], res[:, core_rows(kk)], NN)

    def plane_next(j):
        if j < Z:
            arrived(piece(j, y, x), az, (Z - j,))
            plane_start(j)

    v[z, pl.ds(pl.multiple_of(k * side + y * block + x * n, n), n), :] = items[0]
    own = piece(0, y, x)
    plane_start(0)
    for d in range(1, Z):
        send(own, own, az, (d,), zdev(d))
    forward(0)
    plane_next(1)
    load_u.wait()
    ut[...] = jnp.transpose(u[...])
    share(0)
    plane_next(2)
    forward(1)
    shared(0)
    plane_next(3)
    load_tiles.wait()
    for j in range(Z):
        last = j == Z - 1
        residuals(j)
        if not last:
            share(j + 1)
        if j + 2 < Z:
            forward(j + 2)
        if j > 0:
            reduce_first(j - 1)
        gsend[j] = item_part(1 - k).astype(jnp.bfloat16)
        send(gsend.at[j], grecv.at[j], gc, (j,), sibling)
        if j > 1:
            reduce_third(j - 2)
        gkept[j] = item_part(k)
        if not last:
            region_part(j)
            if j > 0:
                reduce_second(j - 1)
            shared(j + 1)
    reduce_first(Z - 1)
    reduce_second(Z - 2)
    region_part(Z - 1)
    reduce_second(Z - 1)
    reduce_third(Z - 2)
    reduce_third(Z - 1)
    total = acc[...]
    for j in range(1, Z):
        arrived(r_z.at[j - 1], gz, (j,))
        total = total + r_z[j - 1].astype(jnp.float32)
    wide = items[0].astype(jnp.float32)
    new_items[0] = wide - item_rate * (total + decay_rate * wide)
    for copy in sent:
        copy.wait_send()


def on_device(R, Z, Y, region_factors, item_factors, slab_blocks, block_rows, counts):
    bf16, f32 = jnp.bfloat16, jnp.float32
    height, width = region_factors.shape
    _, panels, slots, block, _ = slab_blocks.shape
    n, half, side = block // R, width // 2, Y * block
    chunk = height
    dma = pltpu.SemaphoreType.DMA
    vmem = pltpu.VMEM
    buffers = [
        vmem((height, width), bf16),
        vmem((panels, slots, block, block), bf16),
        vmem((Z, CORES * side, width), bf16),
        vmem((height, CORES * side), bf16),
        vmem((width, height), bf16),
        vmem((Z, width, side), f32),
        vmem((Z, side, width), f32),
        vmem((Z, width, side), bf16),
        vmem((Z, width, side), bf16),
        vmem((Z, Y - 1, (R - 1) * n, half), bf16),
        vmem((Z, Y - 1, (R - 1) * n, half), bf16),
        vmem((Z, R - 1, (Y - 1) * n, half), bf16),
        vmem((Z, R - 1, (Y - 1) * n, half), bf16),
        vmem((Z, R - 1, n, width), bf16),
        vmem((Z, R - 1, n, width), bf16),
        vmem((Z, Y - 1, n, width), bf16),
        vmem((Z, Y - 1, n, width), bf16),
        vmem((Z - 1, n, width), bf16),
        vmem((Z - 1, n, width), bf16),
        vmem((n, width), f32),
    ]
    semaphores = [
        dma((2,)),
        dma((2, Z)),
        dma((2, Z, R)),
        dma((2, Z, Y)),
        dma((2, Z, R, Y)),
        dma((2, Z, R, Y)),
        dma((2, Z)),
        dma((2, Z)),
        dma((2, Z, Y)),
        dma((2, Z, R)),
        dma((2, Z, R)),
        dma((2, Z, Y)),
        dma((2, Z)),
    ]
    region_grad, new_items = pl.pallas_call(
        functools.partial(kernel, R, Z, Y, chunk),
        out_shape=(pltpu.VMEM((height, width), f32), pltpu.VMEM(item_factors.shape, f32)),
        in_specs=[
            pl.BlockSpec(memory_space=pltpu.VMEM),
            pl.BlockSpec(memory_space=pltpu.HBM),
            pl.BlockSpec(memory_space=pltpu.HBM),
            pl.BlockSpec(memory_space=pltpu.SMEM),
            pl.BlockSpec(memory_space=pltpu.SMEM),
        ],
        out_specs=(pl.BlockSpec(memory_space=pltpu.VMEM), pl.BlockSpec(memory_space=pltpu.VMEM)),
        scratch_shapes=buffers + semaphores,
        compiler_params=pltpu.CompilerParams(
            collective_id=0, has_side_effects=True, vmem_limit_bytes=56 * 1024 * 1024),
        cost_estimate=pl.CostEstimate(
            flops=6 * height * panels * block * width, bytes_accessed=8 * height * width, transcendentals=0),
    )(item_factors, region_factors, slab_blocks, jnp.transpose(block_rows, (2, 0, 1)), counts)
    wide = region_factors.astype(f32)
    return wide - region_rate * (region_grad + decay_rate * wide), new_items


def solution(mesh):
    R, C = mesh.shape["row"], mesh.shape["col"]
    chips = C // CORES
    Z = 4
    Y = chips // Z
    return jax.shard_map(
        functools.partial(on_device, R, Z, Y),
        mesh=mesh,
        in_specs=(
            P(("row", "col"), None),
            P("col", "row", None),
            P(("row", "col"), None, None, None, None),
            P(("row", "col"), None, None),
            P(("row", "col"), None),
        ),
        out_specs=(P(("row", "col"), None), P("col", "row", None)),
        check_vma=False,
    )
```

```python
import functools

import jax
import jax.numpy as jnp
from jax import lax
from jax.experimental import pallas as pl
from jax.experimental.pallas import tpu as pltpu
from jax.sharding import PartitionSpec as P

region_rate = 0.05
item_rate = 0.01
decay_rate = 0.1

MESH = pl.DeviceIdType.MESH
CORES = 2
NT = (((1,), (1,)), ((), ()))
NN = (((1,), (0,)), ((), ()))


def mm(a, b, dims):
    return lax.dot_general(a, b, dims, preferred_element_type=jnp.float32)


def kernel(R, Z, Y, chunk, items, regions, slab, rows, counts, region_grad, new_items,
           u, tiles, v, res, ut, gkept, gown, gsend, grecv,
           s_a, r_a, s_b, r_b, s_x, r_x, s_y, r_y, s_z, r_z, acc,
           places, loc_sem, az, ax, ay, aa, ab, sib, gc, ga, gb, gx, gy, gz):
    x = lax.axis_index("row")
    c = lax.axis_index("col")
    k = lax.rem(c, CORES)
    y = lax.rem(c // CORES, Y)
    z = c // (CORES * Y)
    block = tiles.shape[-1]
    width = u.shape[-1]
    half = width // 2
    n = block // R
    slots = tiles.shape[1]

    def col_of(zz, yy, kk):
        return (zz * Y + yy) * CORES + kk

    def xdev(d):
        return {"row": lax.rem(x + d, R), "col": c}

    def ydev(d):
        return {"row": x, "col": col_of(z, lax.rem(y + d, Y), k)}

    def zdev(d):
        return {"row": x, "col": col_of(lax.rem(z + d, Z), y, k)}

    sibling = {"row": x, "col": col_of(z, y, 1 - k)}
    peers = [xdev(d) for d in range(1, R)] + [ydev(d) for d in range(1, Y)] + [zdev(d) for d in range(1, Z)] + [sibling]

    load_u = pltpu.make_async_copy(regions, u, loc_sem.at[0])
    load_u.start()
    load_tiles = pltpu.make_async_copy(slab.at[0], tiles, loc_sem.at[1])
    load_tiles.start()

    barrier = pltpu.get_barrier_semaphore()
    for peer in peers:
        pl.semaphore_signal(barrier, inc=1, device_id=peer, device_id_type=MESH)
    pl.semaphore_wait(barrier, len(peers))

    sent = []

    def remote(src, dst, sems, index, device):
        return pltpu.make_async_remote_copy(
            src_ref=src, dst_ref=dst, send_sem=sems.at[(0,) + index], recv_sem=sems.at[(1,) + index],
            device_id=device, device_id_type=MESH)

    def send(src, dst, sems, index, device):
        copy = remote(src, dst, sems, index, device)
        copy.start()
        sent.append(copy)

    def arrived(dst, sems, index):
        remote(dst, dst, sems, index, sibling).wait_recv()

    def zslot(j):
        return lax.rem(z + j, Z)

    def xback(d):
        return lax.rem(x + R - d, R)

    def yback(d):
        return lax.rem(y + Y - d, Y)

    side = Y * block

    def at_row(yy, xx):
        return pl.ds(pl.multiple_of(yy * block + xx * n, n), n)

    def core_rows(kk):
        return pl.ds(pl.multiple_of(kk * side, side), side)

    def piece(j, yy, xx, columns=slice(None)):
        return v.at[zslot(j), pl.ds(pl.multiple_of(k * side + yy * block + xx * n, n), n), columns]

    first, second = pl.ds(0, half), pl.ds(half, half)

    def plane_start(j):
        own = piece(j, y, x)
        for d in range(1, R):
            send(own, own, ax, (j, d), xdev(d))
        for d in range(1, Y):
            send(own, own, ay, (j, d), ydev(d))

    def forward(j):
        for dx in range(1, R):
            arrived(piece(j, y, xback(dx)), ax, (j, dx))
            part = piece(j, y, xback(dx), first)
            for dy in range(1, Y):
                send(part, part, aa, (j, dx, dy), ydev(dy))
        for dy in range(1, Y):
            arrived(piece(j, yback(dy), x), ay, (j, dy))
            part = piece(j, yback(dy), x, second)
            for dx in range(1, R):
                send(part, part, ab, (j, dx, dy), xdev(dx))

    def share(j):
        for dx in range(1, R):
            for dy in range(1, Y):
                arrived(piece(j, yback(dy), xback(dx), first), aa, (j, dx, dy))
                arrived(piece(j, yback(dy), xback(dx), second), ab, (j, dx, dy))
        mine = v.at[zslot(j), core_rows(k)]
        send(mine, mine, sib, (j,), sibling)

    def shared(j):
        arrived(v.at[zslot(j), core_rows(1 - k)], sib, (j,))

    def find_places():
        def body(p, carry):
            count = counts[0, p]
            listed = [jnp.where(count > s, rows[s, 0, p], -1) for s in range(slots)]
            for b in range(places.shape[1]):
                found = jnp.int32(0)
                for s in range(slots):
                    found = jnp.where(listed[s] == b, s + 1, found)
                places[p, b] = found
            return carry

        lax.fori_loop(0, places.shape[0], body, 0)

    def residuals(j):
        zz = zslot(j)

        def body(i, carry):
            start = pl.multiple_of(i * chunk, chunk)
            predicted = mm(u[pl.ds(start, chunk), :], v[zz], NT)
            for kk in range(CORES):
                for yy in range(Y):
                    left = (kk * Y + yy) * block
                    p = col_of(zz, yy, kk)
                    for part in range(chunk // block):
                        b = i * (chunk // block) + part
                        found = places[p, b]
                        live = jnp.where(found > 0, jnp.float32(1), jnp.float32(0))
                        tile = tiles[p, jnp.maximum(found - 1, 0)].astype(jnp.float32)
                        pred = predicted[part * block:(part + 1) * block, left:left + block]
                        res[pl.ds(pl.multiple_of(start + part * block, block), block), left:left + block] = (
                            (pred - tile) * live).astype(jnp.bfloat16)
            return carry

        lax.fori_loop(0, u.shape[0] // chunk, body, 0)

    def region_part(j):
        zz = zslot(j)

        def body(i, carry):
            here = pl.ds(pl.multiple_of(i * chunk, chunk), chunk)
            total = mm(res[here, :], v[zz], NN)
            if j > 0:
                total = total + region_grad[here, :]
            region_grad[here, :] = total
            return carry

        lax.fori_loop(0, u.shape[0] // chunk, body, 0)

    def reduce_first(j):
        arrived(grecv.at[j], gc, (j,))
        gown[j] = jnp.transpose(gkept[j] + grecv[j])
        for dy in range(1, Y):
            yy = lax.rem(y + dy, Y)
            for dx in range(1, R):
                s_a[j, dy - 1, (dx - 1) * n:dx * n, :] = gown[j, at_row(yy, lax.rem(x + dx, R)), :half].astype(jnp.bfloat16)
            send(s_a.at[j, dy - 1], r_a.at[j, dy - 1], ga, (j, dy), ydev(dy))
        for dx in range(1, R):
            xx = lax.rem(x + dx, R)
            for dy in range(1, Y):
                s_b[j, dx - 1, (dy - 1) * n:dy * n, :] = gown[j, at_row(lax.rem(y + dy, Y), xx), half:].astype(jnp.bfloat16)
            send(s_b.at[j, dx - 1], r_b.at[j, dx - 1], gb, (j, dx), xdev(dx))

    def reduce_second(j):
        for dy in range(1, Y):
            arrived(r_a.at[j, dy - 1], ga, (j, dy))
        for dx in range(1, R):
            here = at_row(y, lax.rem(x + dx, R))
            total = gown[j, here, :half]
            for dy in range(1, Y):
                total = total + r_a[j, dy - 1, (dx - 1) * n:dx * n, :].astype(jnp.float32)
            s_x[j, dx - 1, :, :half] = total.astype(jnp.bfloat16)
            s_x[j, dx - 1, :, half:] = gown[j, here, half:].astype(jnp.bfloat16)
            send(s_x.at[j, dx - 1], r_x.at[j, dx - 1], gx, (j, dx), xdev(dx))
        for dx in range(1, R):
            arrived(r_b.at[j, dx - 1], gb, (j, dx))
        for dy in range(1, Y):
            here = at_row(lax.rem(y + dy, Y), x)
            total = gown[j, here, half:]
            for dx in range(1, R):
                total = total + r_b[j, dx - 1, (dy - 1) * n:dy * n, :].astype(jnp.float32)
            s_y[j, dy - 1, :, half:] = total.astype(jnp.bfloat16)
            s_y[j, dy - 1, :, :half] = gown[j, here, :half].astype(jnp.bfloat16)
            send(s_y.at[j, dy - 1], r_y.at[j, dy - 1], gy, (j, dy), ydev(dy))

    def reduce_third(j):
        total = gown[j, at_row(y, x), :]
        for dx in range(1, R):
            arrived(r_x.at[j, dx - 1], gx, (j, dx))
            total = total + r_x[j, dx - 1].astype(jnp.float32)
        for dy in range(1, Y):
            arrived(r_y.at[j, dy - 1], gy, (j, dy))
            total = total + r_y[j, dy - 1].astype(jnp.float32)
        if j == 0:
            acc[...] = total
        else:
            s_z[j - 1] = total.astype(jnp.bfloat16)
            send(s_z.at[j - 1], r_z.at[j - 1], gz, (j,), zdev(j))

    def item_part(kk):
        return mm(ut[...], res[:, core_rows(kk)], NN)

    def plane_next(j):
        if j < Z:
            arrived(piece(j, y, x), az, (Z - j,))
            plane_start(j)

    v[z, pl.ds(pl.multiple_of(k * side + y * block + x * n, n), n), :] = items[0]
    own = piece(0, y, x)
    plane_start(0)
    for d in range(1, Z):
        send(own, own, az, (d,), zdev(d))
    find_places()
    forward(0)
    plane_next(1)
    load_u.wait()
    ut[...] = jnp.transpose(u[...])
    share(0)
    plane_next(2)
    forward(1)
    shared(0)
    plane_next(3)
    load_tiles.wait()
    for j in range(Z):
        last = j == Z - 1
        residuals(j)
        if not last:
            share(j + 1)
        if j + 2 < Z:
            forward(j + 2)
        if j > 0:
            reduce_first(j - 1)
        gsend[j] = item_part(1 - k)
        send(gsend.at[j], grecv.at[j], gc, (j,), sibling)
        if j > 1:
            reduce_third(j - 2)
        gkept[j] = item_part(k)
        if not last:
            region_part(j)
            if j > 0:
                reduce_second(j - 1)
            shared(j + 1)
    reduce_first(Z - 1)
    reduce_second(Z - 2)
    region_part(Z - 1)
    reduce_second(Z - 1)
    reduce_third(Z - 2)
    reduce_third(Z - 1)
    total = acc[...]
    for j in range(1, Z):
        arrived(r_z.at[j - 1], gz, (j,))
        total = total + r_z[j - 1].astype(jnp.float32)
    wide = items[0].astype(jnp.float32)
    new_items[0] = wide - item_rate * (total + decay_rate * wide)
    for copy in sent:
        copy.wait_send()


def on_device(R, Z, Y, region_factors, item_factors, slab_blocks, block_rows, counts):
    bf16, f32 = jnp.bfloat16, jnp.float32
    height, width = region_factors.shape
    _, panels, slots, block, _ = slab_blocks.shape
    n, half, side = block // R, width // 2, Y * block
    chunk = height
    dma = pltpu.SemaphoreType.DMA
    vmem = pltpu.VMEM
    buffers = [
        vmem((height, width), bf16),
        vmem((panels, slots, block, block), bf16),
        vmem((Z, CORES * side, width), bf16),
        vmem((height, CORES * side), bf16),
        vmem((width, height), bf16),
        vmem((Z, width, side), f32),
        vmem((Z, side, width), f32),
        vmem((Z, width, side), f32),
        vmem((Z, width, side), f32),
        vmem((Z, Y - 1, (R - 1) * n, half), bf16),
        vmem((Z, Y - 1, (R - 1) * n, half), bf16),
        vmem((Z, R - 1, (Y - 1) * n, half), bf16),
        vmem((Z, R - 1, (Y - 1) * n, half), bf16),
        vmem((Z, R - 1, n, width), bf16),
        vmem((Z, R - 1, n, width), bf16),
        vmem((Z, Y - 1, n, width), bf16),
        vmem((Z, Y - 1, n, width), bf16),
        vmem((Z - 1, n, width), bf16),
        vmem((Z - 1, n, width), bf16),
        vmem((n, width), f32),
    ]
    small = [
        pltpu.SMEM((panels, height // block), jnp.int32),
        dma((2,)),
        dma((2, Z)),
        dma((2, Z, R)),
        dma((2, Z, Y)),
        dma((2, Z, R, Y)),
        dma((2, Z, R, Y)),
        dma((2, Z)),
        dma((2, Z)),
        dma((2, Z, Y)),
        dma((2, Z, R)),
        dma((2, Z, R)),
        dma((2, Z, Y)),
        dma((2, Z)),
    ]
    region_grad, new_items = pl.pallas_call(
        functools.partial(kernel, R, Z, Y, chunk),
        out_shape=(pltpu.VMEM((height, width), f32), pltpu.VMEM(item_factors.shape, f32)),
        in_specs=[
            pl.BlockSpec(memory_space=pltpu.VMEM),
            pl.BlockSpec(memory_space=pltpu.HBM),
            pl.BlockSpec(memory_space=pltpu.HBM),
            pl.BlockSpec(memory_space=pltpu.SMEM),
            pl.BlockSpec(memory_space=pltpu.SMEM),
        ],
        out_specs=(pl.BlockSpec(memory_space=pltpu.VMEM), pl.BlockSpec(memory_space=pltpu.VMEM)),
        scratch_shapes=buffers + small,
        compiler_params=pltpu.CompilerParams(
            collective_id=0, has_side_effects=True, vmem_limit_bytes=56 * 1024 * 1024),
        cost_estimate=pl.CostEstimate(
            flops=6 * height * panels * block * width, bytes_accessed=8 * height * width, transcendentals=0),
    )(item_factors, region_factors, slab_blocks, jnp.transpose(block_rows, (2, 0, 1)), counts)
    wide = region_factors.astype(f32)
    return wide - region_rate * (region_grad + decay_rate * wide), new_items


def solution(mesh):
    R, C = mesh.shape["row"], mesh.shape["col"]
    chips = C // CORES
    Z = 4
    Y = chips // Z
    return jax.shard_map(
        functools.partial(on_device, R, Z, Y),
        mesh=mesh,
        in_specs=(
            P(("row", "col"), None),
            P("col", "row", None),
            P(("row", "col"), None, None, None, None),
            P(("row", "col"), None, None),
            P(("row", "col"), None),
        ),
        out_specs=(P(("row", "col"), None), P("col", "row", None)),
        check_vma=False,
    )
```

```python
import functools

import jax
import jax.numpy as jnp
from jax import lax
from jax.experimental import pallas as pl
from jax.experimental.pallas import tpu as pltpu
from jax.sharding import PartitionSpec as P

region_rate = 0.05
item_rate = 0.01
decay_rate = 0.1

MESH = pl.DeviceIdType.MESH
CORES = 2
NT = (((1,), (1,)), ((), ()))
NN = (((1,), (0,)), ((), ()))


def mm(a, b, dims):
    return lax.dot_general(a, b, dims, preferred_element_type=jnp.float32)


def kernel(R, Z, Y, chunk, items, regions, slab, rows, counts, region_grad, new_items,
           u, tiles, v, res, ut, gkept, gown, gsend, grecv,
           s_a, r_a, s_b, r_b, s_x, r_x, s_y, r_y, s_z, r_z, acc,
           places, loc_sem, az, ax, ay, aa, ab, sib, gc, ga, gb, gx, gy, gz):
    x = lax.axis_index("row")
    c = lax.axis_index("col")
    k = lax.rem(c, CORES)
    y = lax.rem(c // CORES, Y)
    z = c // (CORES * Y)
    block = tiles.shape[-1]
    width = u.shape[-1]
    half = width // 2
    n = block // R
    slots = tiles.shape[1]

    def col_of(zz, yy, kk):
        return (zz * Y + yy) * CORES + kk

    def xdev(d):
        return {"row": lax.rem(x + d, R), "col": c}

    def ydev(d):
        return {"row": x, "col": col_of(z, lax.rem(y + d, Y), k)}

    def zdev(d):
        return {"row": x, "col": col_of(lax.rem(z + d, Z), y, k)}

    sibling = {"row": x, "col": col_of(z, y, 1 - k)}
    peers = [xdev(d) for d in range(1, R)] + [ydev(d) for d in range(1, Y)] + [zdev(d) for d in range(1, Z)] + [sibling]

    load_u = pltpu.make_async_copy(regions, u, loc_sem.at[0])
    load_u.start()
    load_tiles = pltpu.make_async_copy(slab.at[0], tiles, loc_sem.at[1])
    load_tiles.start()

    barrier = pltpu.get_barrier_semaphore()
    for peer in peers:
        pl.semaphore_signal(barrier, inc=1, device_id=peer, device_id_type=MESH)
    pl.semaphore_wait(barrier, len(peers))

    sent = []

    def remote(src, dst, sems, index, device):
        return pltpu.make_async_remote_copy(
            src_ref=src, dst_ref=dst, send_sem=sems.at[(0,) + index], recv_sem=sems.at[(1,) + index],
            device_id=device, device_id_type=MESH)

    def send(src, dst, sems, index, device):
        copy = remote(src, dst, sems, index, device)
        copy.start()
        sent.append(copy)

    def arrived(dst, sems, index):
        remote(dst, dst, sems, index, sibling).wait_recv()

    def zslot(j):
        return lax.rem(z + j, Z)

    def xback(d):
        return lax.rem(x + R - d, R)

    def yback(d):
        return lax.rem(y + Y - d, Y)

    side = Y * block

    def at_row(yy, xx):
        return pl.ds(pl.multiple_of(yy * block + xx * n, n), n)

    def core_rows(kk):
        return pl.ds(pl.multiple_of(kk * side, side), side)

    def piece(j, yy, xx, columns=slice(None)):
        return v.at[zslot(j), pl.ds(pl.multiple_of(k * side + yy * block + xx * n, n), n), columns]

    first, second = pl.ds(0, half), pl.ds(half, half)

    def plane_start(j):
        own = piece(j, y, x)
        for d in range(1, R):
            send(own, own, ax, (j, d), xdev(d))
        for d in range(1, Y):
            send(own, own, ay, (j, d), ydev(d))

    def forward(j):
        for dx in range(1, R):
            arrived(piece(j, y, xback(dx)), ax, (j, dx))
            part = piece(j, y, xback(dx), first)
            for dy in range(1, Y):
                send(part, part, aa, (j, dx, dy), ydev(dy))
        for dy in range(1, Y):
            arrived(piece(j, yback(dy), x), ay, (j, dy))
            part = piece(j, yback(dy), x, second)
            for dx in range(1, R):
                send(part, part, ab, (j, dx, dy), xdev(dx))

    def share(j):
        for dx in range(1, R):
            for dy in range(1, Y):
                arrived(piece(j, yback(dy), xback(dx), first), aa, (j, dx, dy))
                arrived(piece(j, yback(dy), xback(dx), second), ab, (j, dx, dy))
        mine = v.at[zslot(j), core_rows(k)]
        send(mine, mine, sib, (j,), sibling)

    def shared(j):
        arrived(v.at[zslot(j), core_rows(1 - k)], sib, (j,))

    def find_places():
        def body(p, carry):
            count = counts[0, p]
            listed = [jnp.where(count > s, rows[s, 0, p], -1) for s in range(slots)]
            for b in range(places.shape[1]):
                found = jnp.int32(0)
                for s in range(slots):
                    found = jnp.where(listed[s] == b, s + 1, found)
                places[p, b] = found
            return carry

        lax.fori_loop(0, places.shape[0], body, 0)

    def residuals(j):
        zz = zslot(j)

        def body(i, carry):
            start = pl.multiple_of(i * chunk, chunk)
            predicted = mm(u[pl.ds(start, chunk), :], v[zz], NT)
            for kk in range(CORES):
                for yy in range(Y):
                    left = (kk * Y + yy) * block
                    p = col_of(zz, yy, kk)
                    for part in range(chunk // block):
                        b = i * (chunk // block) + part
                        found = places[p, b]
                        live = jnp.where(found > 0, jnp.float32(1), jnp.float32(0))
                        tile = tiles[p, jnp.maximum(found - 1, 0)].astype(jnp.float32)
                        pred = predicted[part * block:(part + 1) * block, left:left + block]
                        res[pl.ds(pl.multiple_of(start + part * block, block), block), left:left + block] = (
                            (pred - tile) * live).astype(jnp.bfloat16)
            return carry

        lax.fori_loop(0, u.shape[0] // chunk, body, 0)

    def region_part(j):
        zz = zslot(j)

        def body(i, carry):
            here = pl.ds(pl.multiple_of(i * chunk, chunk), chunk)
            total = mm(res[here, :], v[zz], NN)
            if j > 0:
                total = total + region_grad[here, :]
            region_grad[here, :] = total
            return carry

        lax.fori_loop(0, u.shape[0] // chunk, body, 0)

    def reduce_first(j):
        arrived(grecv.at[j], gc, (j,))
        gown[j] = jnp.transpose(gkept[j] + grecv[j])
        for dy in range(1, Y):
            yy = lax.rem(y + dy, Y)
            for dx in range(1, R):
                s_a[j, dy - 1, (dx - 1) * n:dx * n, :] = gown[j, at_row(yy, lax.rem(x + dx, R)), :half].astype(jnp.bfloat16)
            send(s_a.at[j, dy - 1], r_a.at[j, dy - 1], ga, (j, dy), ydev(dy))
        for dx in range(1, R):
            xx = lax.rem(x + dx, R)
            for dy in range(1, Y):
                s_b[j, dx - 1, (dy - 1) * n:dy * n, :] = gown[j, at_row(lax.rem(y + dy, Y), xx), half:].astype(jnp.bfloat16)
            send(s_b.at[j, dx - 1], r_b.at[j, dx - 1], gb, (j, dx), xdev(dx))

    def reduce_second(j):
        for dy in range(1, Y):
            arrived(r_a.at[j, dy - 1], ga, (j, dy))
        for dx in range(1, R):
            here = at_row(y, lax.rem(x + dx, R))
            total = gown[j, here, :half]
            for dy in range(1, Y):
                total = total + r_a[j, dy - 1, (dx - 1) * n:dx * n, :].astype(jnp.float32)
            s_x[j, dx - 1, :, :half] = total.astype(jnp.bfloat16)
            s_x[j, dx - 1, :, half:] = gown[j, here, half:].astype(jnp.bfloat16)
            send(s_x.at[j, dx - 1], r_x.at[j, dx - 1], gx, (j, dx), xdev(dx))
        for dx in range(1, R):
            arrived(r_b.at[j, dx - 1], gb, (j, dx))
        for dy in range(1, Y):
            here = at_row(lax.rem(y + dy, Y), x)
            total = gown[j, here, half:]
            for dx in range(1, R):
                total = total + r_b[j, dx - 1, (dy - 1) * n:dy * n, :].astype(jnp.float32)
            s_y[j, dy - 1, :, half:] = total.astype(jnp.bfloat16)
            s_y[j, dy - 1, :, :half] = gown[j, here, :half].astype(jnp.bfloat16)
            send(s_y.at[j, dy - 1], r_y.at[j, dy - 1], gy, (j, dy), ydev(dy))

    def reduce_third(j):
        total = gown[j, at_row(y, x), :]
        for dx in range(1, R):
            arrived(r_x.at[j, dx - 1], gx, (j, dx))
            total = total + r_x[j, dx - 1].astype(jnp.float32)
        for dy in range(1, Y):
            arrived(r_y.at[j, dy - 1], gy, (j, dy))
            total = total + r_y[j, dy - 1].astype(jnp.float32)
        if j == 0:
            acc[...] = total
        else:
            s_z[j - 1] = total.astype(jnp.bfloat16)
            send(s_z.at[j - 1], r_z.at[j - 1], gz, (j,), zdev(j))

    def item_part(kk):
        return mm(ut[...], res[:, core_rows(kk)], NN)

    def plane_next(j):
        if j < Z:
            arrived(piece(j, y, x), az, (Z - j,))
            plane_start(j)

    v[z, pl.ds(pl.multiple_of(k * side + y * block + x * n, n), n), :] = items[0]
    own = piece(0, y, x)
    plane_start(0)
    for d in range(1, Z):
        send(own, own, az, (d,), zdev(d))
    find_places()
    forward(0)
    plane_next(1)
    load_u.wait()
    ut[...] = jnp.transpose(u[...])
    share(0)
    plane_next(2)
    forward(1)
    shared(0)
    plane_next(3)
    load_tiles.wait()
    for j in range(Z):
        last = j == Z - 1
        residuals(j)
        gsend[j] = item_part(1 - k)
        send(gsend.at[j], grecv.at[j], gc, (j,), sibling)
        gkept[j] = item_part(k)
        if j > 0:
            reduce_second(j - 1)
        if last:
            reduce_first(j)
        region_part(j)
        if not last:
            reduce_first(j)
            share(j + 1)
        if j + 2 < Z:
            forward(j + 2)
        if j > 0:
            reduce_third(j - 1)
        if not last:
            shared(j + 1)
    reduce_second(Z - 1)
    reduce_third(Z - 1)
    total = acc[...]
    for j in range(1, Z):
        arrived(r_z.at[j - 1], gz, (j,))
        total = total + r_z[j - 1].astype(jnp.float32)
    wide = items[0].astype(jnp.float32)
    new_items[0] = wide - item_rate * (total + decay_rate * wide)
    for copy in sent:
        copy.wait_send()


def on_device(R, Z, Y, region_factors, item_factors, slab_blocks, block_rows, counts):
    bf16, f32 = jnp.bfloat16, jnp.float32
    height, width = region_factors.shape
    _, panels, slots, block, _ = slab_blocks.shape
    n, half, side = block // R, width // 2, Y * block
    chunk = height
    dma = pltpu.SemaphoreType.DMA
    vmem = pltpu.VMEM
    buffers = [
        vmem((height, width), bf16),
        vmem((panels, slots, block, block), bf16),
        vmem((Z, CORES * side, width), bf16),
        vmem((height, CORES * side), bf16),
        vmem((width, height), bf16),
        vmem((Z, width, side), f32),
        vmem((Z, side, width), f32),
        vmem((Z, width, side), f32),
        vmem((Z, width, side), f32),
        vmem((Z, Y - 1, (R - 1) * n, half), bf16),
        vmem((Z, Y - 1, (R - 1) * n, half), bf16),
        vmem((Z, R - 1, (Y - 1) * n, half), bf16),
        vmem((Z, R - 1, (Y - 1) * n, half), bf16),
        vmem((Z, R - 1, n, width), bf16),
        vmem((Z, R - 1, n, width), bf16),
        vmem((Z, Y - 1, n, width), bf16),
        vmem((Z, Y - 1, n, width), bf16),
        vmem((Z - 1, n, width), bf16),
        vmem((Z - 1, n, width), bf16),
        vmem((n, width), f32),
    ]
    small = [
        pltpu.SMEM((panels, height // block), jnp.int32),
        dma((2,)),
        dma((2, Z)),
        dma((2, Z, R)),
        dma((2, Z, Y)),
        dma((2, Z, R, Y)),
        dma((2, Z, R, Y)),
        dma((2, Z)),
        dma((2, Z)),
        dma((2, Z, Y)),
        dma((2, Z, R)),
        dma((2, Z, R)),
        dma((2, Z, Y)),
        dma((2, Z)),
    ]
    region_grad, new_items = pl.pallas_call(
        functools.partial(kernel, R, Z, Y, chunk),
        out_shape=(pltpu.VMEM((height, width), f32), pltpu.VMEM(item_factors.shape, f32)),
        in_specs=[
            pl.BlockSpec(memory_space=pltpu.VMEM),
            pl.BlockSpec(memory_space=pltpu.HBM),
            pl.BlockSpec(memory_space=pltpu.HBM),
            pl.BlockSpec(memory_space=pltpu.SMEM),
            pl.BlockSpec(memory_space=pltpu.SMEM),
        ],
        out_specs=(pl.BlockSpec(memory_space=pltpu.VMEM), pl.BlockSpec(memory_space=pltpu.VMEM)),
        scratch_shapes=buffers + small,
        compiler_params=pltpu.CompilerParams(
            collective_id=0, has_side_effects=True, vmem_limit_bytes=56 * 1024 * 1024),
        cost_estimate=pl.CostEstimate(
            flops=6 * height * panels * block * width, bytes_accessed=8 * height * width, transcendentals=0),
    )(item_factors, region_factors, slab_blocks, jnp.transpose(block_rows, (2, 0, 1)), counts)
    wide = region_factors.astype(f32)
    return wide - region_rate * (region_grad + decay_rate * wide), new_items


def solution(mesh):
    R, C = mesh.shape["row"], mesh.shape["col"]
    chips = C // CORES
    Z = 4
    Y = chips // Z
    return jax.shard_map(
        functools.partial(on_device, R, Z, Y),
        mesh=mesh,
        in_specs=(
            P(("row", "col"), None),
            P("col", "row", None),
            P(("row", "col"), None, None, None, None),
            P(("row", "col"), None, None),
            P(("row", "col"), None),
        ),
        out_specs=(P(("row", "col"), None), P("col", "row", None)),
        check_vma=False,
    )
```
